32 devices in a mesh: rows: 8 (over y, x, core), cols: 4 (over z).
Axes of the slice: x: 2, y: 2, z: 4, core: 2. Of those that a mesh axis runs over, the one named last changes fastest.
Arguments:
- features: bfloat16 [64, 256, 512], P('rows', 'cols'), may hold values from -6 to 6
- w_l2l: bfloat16 [3, 3, 128, 128], replicated, may hold values from -0.09375 to 0.09375
- w_g2l: bfloat16 [3, 3, 384, 128], replicated, may hold values from -0.09375 to 0.09375
- w_l2g: bfloat16 [3, 3, 128, 384], replicated, may hold values from -0.1875 to 0.1875
- w_in: bfloat16 [384, 192], replicated, may hold values from -0.3125 to 0.3125
- in_scale: float32 [192], replicated, may hold values from 0.5 to 1.5
- in_shift: float32 [192], replicated, may hold values from -2.5 to 2.5
- w_fu: bfloat16 [384, 384], replicated, may hold values from -0.3125 to 0.3125
- fu_scale: float32 [384], replicated, may hold values from 0.1 to 1.9
- fu_shift: float32 [384], replicated, may hold values from -2.5 to 2.5
- w_out: bfloat16 [192, 384], replicated, may hold values from -0.4375 to 0.4375
- local_scale: float32 [128], replicated, may hold values from 0.5 to 1.5
- local_shift: float32 [128], replicated, may hold values from -2.5 to 2.5
- global_scale: float32 [384], replicated, may hold values from 0.5 to 1.5
- global_shift: float32 [384], replicated, may hold values from -2.5 to 2.5
Outputs:
- out_local: bfloat16 [64, 256, 128], P('rows', 'cols')
- out_global: bfloat16 [64, 256, 384], P('rows', 'cols')
The draws below stay inside these ranges and needn't reach their ends.
All inputs are finite; a program needn't handle non-finite values.
Results may differ from the reference program's by a relative error of at most 0.0085.
Values may be sent and summed in bfloat16 or wider, within the bound.
A program may use at most 64 MiB of HBM per device.

```python
import math
import jax
import jax.numpy as jnp
from jax import lax

CL = 128
CG = 384
CS = 192
ROW_DEV = 8
H = 64
W = 256


def level_of(rng, shape, pieces, least, largest):
    factor_of, own = 1.0, jax.random.fold_in(rng, 6)
    for axis_at, parts in pieces:
        steps = jnp.exp(jax.random.uniform(jax.random.fold_in(own, axis_at), (parts,), jnp.float32, least / len(pieces), largest / len(pieces)))
        factor_of = factor_of * jnp.repeat(steps, shape[axis_at] // parts).reshape([-1 if axis == axis_at else 1 for axis in range(len(shape))])
    return factor_of


def centred(key, dims, scale, reach, pieces=(), kind=jnp.bfloat16):
    values = scale * jax.random.normal(key, dims, jnp.float32)
    if pieces:
        values = values * level_of(key, dims, pieces, -0.22, 0.18)
    return jnp.clip(values, -reach, reach).astype(kind)


def setup_inputs(seed: int = 0) -> dict:
    splits = jax.random.split(jax.random.key(seed), 16)
    features = centred(splits[0], (H, W, CL + CG), 1.0, 6.0, ((0, 8), (1, 4)))
    w_l2l = centred(splits[1], (3, 3, CL, CL), (9 * (CL + CG)) ** -0.5, 0.09375)
    w_g2l = centred(splits[2], (3, 3, CG, CL), (9 * (CL + CG)) ** -0.5, 0.09375)
    w_l2g = centred(splits[3], (3, 3, CL, CG), (9 * CL) ** -0.5, 0.1875)
    w_in = centred(splits[4], (CG, CS), CG ** -0.5, 0.3125)
    in_scale = jnp.clip(1.0 + 0.1 * jax.random.normal(splits[5], (CS,), jnp.float32), 0.5, 1.5)
    in_shift = centred(splits[6], (CS,), 0.5, 2.5, (), jnp.float32)
    w_fu = centred(splits[7], (2 * CS, 2 * CS), (2 * CS) ** -0.5, 0.3125)
    fu_scale = jnp.clip(1.0 + 0.18 * jax.random.normal(splits[8], (2 * CS,), jnp.float32), 0.1, 1.9)
    fu_shift = centred(splits[9], (2 * CS,), 0.5, 2.5, (), jnp.float32)
    w_out = centred(splits[10], (CS, CG), CS ** -0.5, 0.4375)
    local_scale = jnp.clip(1.0 + 0.1 * jax.random.normal(splits[11], (CL,), jnp.float32), 0.5, 1.5)
    local_shift = centred(splits[12], (CL,), 0.5, 2.5, (), jnp.float32)
    global_scale = jnp.clip(1.0 + 0.1 * jax.random.normal(splits[13], (CG,), jnp.float32), 0.5, 1.5)
    global_shift = centred(splits[14], (CG,), 0.5, 2.5, (), jnp.float32)
    return {"features": features, "w_l2l": w_l2l, "w_g2l": w_g2l, "w_l2g": w_l2g, "w_in": w_in, "in_scale": in_scale, "in_shift": in_shift, "w_fu": w_fu, "fu_scale": fu_scale, "fu_shift": fu_shift, "w_out": w_out, "local_scale": local_scale, "local_shift": local_shift, "global_scale": global_scale, "global_shift": global_shift}


def rounded(value):
    return lax.optimization_barrier(value.astype(jnp.bfloat16))


def mirrored(value):
    return jnp.roll(jnp.flip(value, -1), 1, -1)


def reference(features, w_l2l, w_g2l, w_l2g, w_in, in_scale, in_shift, w_fu, fu_scale, fu_shift, w_out, local_scale, local_shift, global_scale, global_shift):
    floating = jnp.float32
    highest = lax.Precision.HIGHEST
    height_total = features.shape[0]
    width_total = features.shape[1]
    half_width = width_total // 2
    padded = jnp.pad(features, ((1, 1), (1, 1), (0, 0)), mode="reflect")
    w_local = jnp.concatenate([w_l2l, w_g2l], axis=2).astype(floating)
    w_cross = w_l2g.astype(floating)
    numbers = ("NHWC", "HWIO", "NHWC")
    starts = (jnp.arange(height_total // ROW_DEV) * ROW_DEV).astype(jnp.int32)
    zero_index = jnp.int32(0)

    def window_at(row_start):
        return lax.dynamic_slice(padded, (row_start, zero_index, zero_index), (ROW_DEV + 2, width_total + 2, CL + CG)).astype(floating)[None]

    def first_pass(row_start):
        window = window_at(row_start)
        local_sum = lax.conv_general_dilated(window, w_local, (1, 1), "VALID", dimension_numbers=numbers, precision=highest)[0]
        local_block = jnp.maximum(local_sum * local_scale + local_shift, 0.0).astype(jnp.bfloat16)
        inner_global = window[0, 1:-1, 1:-1, CL:]
        projected = jnp.einsum("hwi,io->hwo", inner_global, w_in.astype(floating), precision=highest)
        reduced_block = jnp.maximum(projected * in_scale + in_shift, 0.0).astype(jnp.bfloat16)
        return local_block, reduced_block

    local_blocks, reduced_blocks = lax.map(first_pass, starts)
    out_local = local_blocks.reshape(height_total, width_total, CL)
    reduced = reduced_blocks.reshape(height_total, width_total, CS)

    channel_group = math.gcd(CS, 8)
    by_channel = reduced.transpose(2, 0, 1).reshape(CS // channel_group, channel_group, height_total, width_total)

    def forward(channel_block):
        along_width = jnp.fft.rfft(channel_block.astype(floating), axis=2, norm="ortho")
        real_full = jnp.real(along_width)
        width_real = real_full[..., :half_width]
        width_imag = jnp.concatenate([real_full[..., half_width:half_width + 1], jnp.imag(along_width)[..., 1:half_width]], axis=-1)
        width_real = rounded(width_real).astype(floating)
        width_imag = rounded(width_imag).astype(floating)
        spectrum = jnp.fft.fft(width_real + 1j * width_imag, axis=1, norm="ortho")
        return jnp.real(spectrum).astype(jnp.bfloat16), jnp.imag(spectrum).astype(jnp.bfloat16)

    spec_real, spec_imag = lax.map(forward, by_channel)
    spec_real = spec_real.reshape(CS, height_total, half_width)
    spec_imag = spec_imag.reshape(CS, height_total, half_width)

    first_real = spec_real[:, :, 0].astype(floating)
    first_imag = spec_imag[:, :, 0].astype(floating)
    mirror_real = mirrored(first_real)
    mirror_imag = mirrored(first_imag)
    zero_real = ((first_real + mirror_real) * 0.5).astype(jnp.bfloat16)
    zero_imag = ((first_imag - mirror_imag) * 0.5).astype(jnp.bfloat16)
    top_real = ((first_imag + mirror_imag) * 0.5).astype(jnp.bfloat16)
    top_imag = ((mirror_real - first_real) * 0.5).astype(jnp.bfloat16)
    cells_real = jnp.concatenate([zero_real[:, :, None], spec_real[:, :, 1:], top_real[:, :, None]], axis=2)
    cells_imag = jnp.concatenate([zero_imag[:, :, None], spec_imag[:, :, 1:], top_imag[:, :, None]], axis=2)
    column_count = half_width + 1

    def mixing(row_start):
        part_real = lax.dynamic_slice_in_dim(cells_real, row_start, ROW_DEV, 1)
        part_imag = lax.dynamic_slice_in_dim(cells_imag, row_start, ROW_DEV, 1)
        stacked = jnp.stack([part_real, part_imag], axis=-1).transpose(1, 2, 0, 3)
        stacked = stacked.reshape(ROW_DEV * column_count, 2 * CS).astype(floating)
        mixed_cells = jnp.maximum(jnp.dot(stacked, w_fu.astype(floating), precision=highest) * fu_scale + fu_shift, 0.0)
        mixed_cells = mixed_cells.astype(jnp.bfloat16).reshape(ROW_DEV, column_count, CS, 2)
        return mixed_cells.transpose(3, 2, 0, 1)

    mixed_blocks = lax.map(mixing, starts)
    mixed_all = mixed_blocks.transpose(1, 2, 0, 3, 4).reshape(2, CS // channel_group, channel_group, height_total, column_count)

    def inverse(halves):
        block_real, block_imag = halves
        along_rows = jnp.fft.ifft(block_real.astype(floating) + 1j * block_imag.astype(floating), axis=1, norm="ortho")
        real_full = jnp.real(along_rows)
        rows_real = real_full[..., :half_width]
        rows_imag = jnp.concatenate([real_full[..., half_width:half_width + 1], jnp.imag(along_rows)[..., 1:half_width]], axis=-1)
        rows_real = rounded(rows_real).astype(floating)
        rows_imag = rounded(rows_imag).astype(floating)
        full = jnp.concatenate([rows_real[..., :1] + 0j, rows_real[..., 1:] + 1j * rows_imag[..., 1:], rows_imag[..., :1] + 0j], axis=-1)
        spatial = jnp.fft.irfft(full, n=width_total, axis=2, norm="ortho")
        return spatial.astype(jnp.bfloat16)

    fourier = lax.map(inverse, (mixed_all[0], mixed_all[1])).reshape(CS, height_total, width_total)

    def second_pass(row_start):
        window = window_at(row_start)
        cross_sum = lax.conv_general_dilated(window[..., :CL], w_cross, (1, 1), "VALID", dimension_numbers=numbers, precision=highest)[0]
        reduced_part = lax.dynamic_slice_in_dim(reduced, row_start, ROW_DEV, 0).astype(floating)
        fourier_part = lax.dynamic_slice_in_dim(fourier, row_start, ROW_DEV, 1).transpose(1, 2, 0).astype(floating)
        joined = rounded(reduced_part + fourier_part).astype(floating)
        projection = jnp.dot(joined.reshape(-1, CS), w_out.astype(floating), precision=highest)
        global_sum = cross_sum + projection.reshape(ROW_DEV, width_total, CG)
        return jnp.maximum(global_sum * global_scale + global_shift, 0.0).astype(jnp.bfloat16)

    out_global = lax.map(second_pass, starts).reshape(height_total, width_total, CG)
    return out_local, out_global
```

```python
import functools
import math

import jax
import jax.numpy as jnp
import ml_dtypes
import numpy as np
from jax import lax
from jax.experimental import pallas as pl
from jax.experimental.pallas import tpu as pltpu
from jax.sharding import PartitionSpec as P

MESH = pl.DeviceIdType.MESH


def padded_2(x, sides, width):
    for axis, dim in sides:
        size, length = (lax.axis_size(axis), x.shape[dim])
        up = [(i, (i + 1) % size) for i in range(size - 1)]
        down = [(j, i) for i, j in up]
        last = lax.slice_in_dim(x, length - width, length, axis=dim)
        initial = lax.slice_in_dim(x, 0, width, axis=dim)
        before = lax.ppermute(last, axis, up)
        after = lax.ppermute(initial, axis, down)
        x = jnp.concatenate([before, x, after], axis=dim)
    return x


def rounded(value):
    return lax.optimization_barrier(value.astype(jnp.bfloat16))


def mirror_rows(value):
    return jnp.roll(jnp.flip(value, 0), 1, 0)


def angle_grid(count_a, count_b, modulus):
    left_index = lax.broadcasted_iota(jnp.int32, (count_a, count_b), 0)
    right_index = lax.broadcasted_iota(jnp.int32, (count_a, count_b), 1)
    return (left_index * right_index % modulus).astype(jnp.float32) * (2.0 * math.pi / modulus)


def along_rows(stacked, spectral, direction):
    highest = lax.Precision.HIGHEST
    length = stacked.shape[0]
    angles = angle_grid(length, length, length)
    factor = 1.0 / math.sqrt(length)
    cos_part = jnp.einsum("qh,hkc->qkc", jnp.cos(angles), stacked, precision=highest)
    sin_part = jnp.einsum("qh,hkc->qkc", jnp.sin(angles), stacked, precision=highest)
    if direction < 0:
        out_real = cos_part[..., :spectral] + sin_part[..., spectral:]
        out_imag = cos_part[..., spectral:] - sin_part[..., :spectral]
    else:
        out_real = cos_part[..., :spectral] - sin_part[..., spectral:]
        out_imag = cos_part[..., spectral:] + sin_part[..., :spectral]
    return (out_real * factor, out_imag * factor)


def shards(
    features,
    w_l2l,
    w_g2l,
    w_l2g,
    w_in,
    in_scale,
    in_shift,
    w_fu,
    fu_scale,
    fu_shift,
    w_out,
    local_scale,
    local_shift,
    global_scale,
    global_shift,
):
    floating = jnp.float32
    highest = lax.Precision.HIGHEST
    rows_here, cols_here, channels = features.shape
    local_width = w_l2l.shape[2]
    global_width = w_l2g.shape[3]
    spectral = w_in.shape[1]
    row_count = lax.axis_size("rows")
    col_count = lax.axis_size("cols")
    row_slab = rows_here // col_count
    column_total = cols_here * col_count
    half_width = column_total // 2
    row_total = rows_here * row_count
    per_device = half_width // (row_count * col_count)
    width_factor = 1.0 / math.sqrt(column_total)
    padded = padded_2(features, (("rows", 0), ("cols", 1)), 1)
    at_top = lax.axis_index("rows") == 0
    at_bottom = lax.axis_index("rows") == row_count - 1
    at_left = lax.axis_index("cols") == 0
    at_right = lax.axis_index("cols") == col_count - 1
    is_first = jnp.logical_and(at_top, at_left)
    padded = padded.at[0].set(jnp.where(at_top, padded[2], padded[0]))
    padded = padded.at[-1].set(jnp.where(at_bottom, padded[-3], padded[-1]))
    padded = padded.at[:, 0].set(jnp.where(at_left, padded[:, 2], padded[:, 0]))
    padded = padded.at[:, -1].set(jnp.where(at_right, padded[:, -3], padded[:, -1]))
    projected = jnp.einsum(
        "hwi,io->hwo", features[..., local_width:], w_in, preferred_element_type=floating
    )
    reduced = rounded(jnp.maximum(projected * in_scale + in_shift, 0.0))
    spread = lax.all_to_all(
        reduced.reshape(col_count, row_slab, cols_here, spectral),
        "cols",
        split_axis=0,
        concat_axis=2,
        tiled=True,
    )
    spread = spread.reshape(row_slab, column_total, spectral)
    pixel_index = lax.broadcasted_iota(jnp.int32, (column_total, half_width), 0)
    freq_index = lax.broadcasted_iota(jnp.int32, (column_total, half_width), 1)
    alternate = jnp.where(pixel_index % 2 == 0, 1.0, -1.0).astype(floating)
    forward_angles = angle_grid(column_total, half_width, column_total)
    forward_cos = jnp.cos(forward_angles)
    forward_sin = jnp.where(freq_index == 0, alternate, -jnp.sin(forward_angles))
    spread_float = spread.astype(floating)
    width_real = (
        jnp.einsum("hwc,wk->hkc", spread_float, forward_cos, precision=highest) * width_factor
    )
    width_imag = (
        jnp.einsum("hwc,wk->hkc", spread_float, forward_sin, precision=highest) * width_factor
    )
    width_spec = jnp.concatenate([width_real, width_imag], axis=-1).astype(jnp.bfloat16)
    width_spec = width_spec.reshape(1, row_slab, row_count, col_count, per_device, 2 * spectral)
    gathered = lax.all_to_all(
        lax.all_to_all(width_spec, "rows", split_axis=2, concat_axis=0, tiled=True),
        "cols",
        split_axis=3,
        concat_axis=1,
        tiled=True,
    )
    w_local = jnp.concatenate([w_l2l, w_g2l], axis=2)
    local_total = jnp.zeros((rows_here * cols_here, local_width), floating)
    cross_total = jnp.zeros((rows_here * cols_here, global_width), floating)
    for row_step in range(3):
        for col_step in range(3):
            window = padded[
                row_step : row_step + rows_here, col_step : col_step + cols_here
            ].reshape(-1, channels)
            local_total = local_total + jnp.dot(
                window, w_local[row_step, col_step], preferred_element_type=floating
            )
            cross_total = cross_total + jnp.dot(
                window[:, :local_width], w_l2g[row_step, col_step], preferred_element_type=floating
            )
    out_local = jnp.maximum(local_total * local_scale + local_shift, 0.0).astype(jnp.bfloat16)
    out_local = out_local.reshape(rows_here, cols_here, local_width)
    columns = gathered.reshape(row_total, per_device, 2 * spectral).astype(floating)
    spec_real, spec_imag = along_rows(columns, spectral, -1.0)
    spec_real = rounded(spec_real)
    spec_imag = rounded(spec_imag)
    first_real = spec_real[:, 0].astype(floating)
    first_imag = spec_imag[:, 0].astype(floating)
    mirror_real = mirror_rows(first_real)
    mirror_imag = mirror_rows(first_imag)
    zero_real = rounded((first_real + mirror_real) * 0.5)
    zero_imag = rounded((first_imag - mirror_imag) * 0.5)
    top_real = rounded((first_imag + mirror_imag) * 0.5)
    top_imag = rounded((mirror_real - first_real) * 0.5)
    lead_real = jnp.where(is_first, zero_real, spec_real[:, 0])
    lead_imag = jnp.where(is_first, zero_imag, spec_imag[:, 0])
    all_real = jnp.concatenate([lead_real[:, None], spec_real[:, 1:], top_real[:, None]], axis=1)
    all_imag = jnp.concatenate([lead_imag[:, None], spec_imag[:, 1:], top_imag[:, None]], axis=1)
    cells = jnp.concatenate([all_real, all_imag], axis=-1).reshape(
        row_total * (per_device + 1), 2 * spectral
    )
    reorder = jnp.concatenate([jnp.arange(spectral) * 2, jnp.arange(spectral) * 2 + 1])
    w_mix = w_fu[reorder][:, reorder]
    mixed_cells = rounded(
        jnp.maximum(
            jnp.dot(cells, w_mix, preferred_element_type=floating) * fu_scale[reorder]
            + fu_shift[reorder],
            0.0,
        )
    )
    mixed_grid = mixed_cells.reshape(row_total, per_device + 1, 2 * spectral).astype(floating)
    low_real = mixed_grid[:, 0, :spectral]
    low_imag = mixed_grid[:, 0, spectral:]
    high_real = mixed_grid[:, per_device, :spectral]
    high_imag = mixed_grid[:, per_device, spectral:]
    joint_real = (low_real + mirror_rows(low_real) - high_imag + mirror_rows(high_imag)) * 0.5
    joint_imag = (low_imag - mirror_rows(low_imag) + high_real + mirror_rows(high_real)) * 0.5
    joint = jnp.concatenate([joint_real, joint_imag], axis=-1)
    lead = jnp.where(is_first, joint, mixed_grid[:, 0])
    into = jnp.concatenate([lead[:, None], mixed_grid[:, 1:per_device]], axis=1)
    back_real, back_imag = along_rows(into, spectral, 1.0)
    back_rows = jnp.concatenate([back_real, back_imag], axis=-1).astype(jnp.bfloat16)
    back_rows = back_rows.reshape(row_total, 1, 1, per_device, 2 * spectral)
    returned = lax.all_to_all(
        lax.all_to_all(back_rows, "rows", split_axis=0, concat_axis=1, tiled=True),
        "cols",
        split_axis=0,
        concat_axis=2,
        tiled=True,
    )
    rows_grid = returned.reshape(row_slab, half_width, 2 * spectral).astype(floating)
    back_freq = lax.broadcasted_iota(jnp.int32, (half_width, column_total), 0)
    back_pixel = lax.broadcasted_iota(jnp.int32, (half_width, column_total), 1)
    back_alternate = jnp.where(back_pixel % 2 == 0, 1.0, -1.0).astype(floating)
    back_angles = angle_grid(half_width, column_total, column_total)
    back_cos = jnp.where(back_freq == 0, 1.0, 2.0 * jnp.cos(back_angles))
    back_sin = jnp.where(back_freq == 0, -back_alternate, 2.0 * jnp.sin(back_angles))
    fourier_real = jnp.einsum("hkc,kw->hwc", rows_grid[..., :spectral], back_cos, precision=highest)
    fourier_real = fourier_real - jnp.einsum(
        "hkc,kw->hwc", rows_grid[..., spectral:], back_sin, precision=highest
    )
    fourier = rounded(fourier_real * width_factor)
    joined = rounded(spread.astype(floating) + fourier.astype(floating))
    terms = jnp.einsum("hwc,co->hwo", joined, w_out, preferred_element_type=floating)
    terms = terms.reshape(row_slab, col_count, cols_here, global_width)
    projection = (
        lax.all_to_all(terms.astype(jnp.bfloat16), "cols", split_axis=1, concat_axis=0, tiled=True)
        .astype(terms.dtype)
        .reshape(rows_here, cols_here, global_width)
    )
    global_sum = cross_total.reshape(rows_here, cols_here, global_width) + projection
    out_global = jnp.maximum(global_sum * global_scale + global_shift, 0.0).astype(jnp.bfloat16)
    return (out_local, out_global)


def tables(rows, cols, height, width, pad_k):
    count = rows * cols
    cell = width // count
    half = width // 2
    freq = np.arange(count)[:, None]
    line = np.arange(height)[None, :]
    turn = 2.0 * np.pi * ((freq * line) % height) / height
    row_cos = np.cos(turn)
    row_sin = -np.sin(turn)
    row_sin[0] = 1.0 - 2.0 * (np.arange(height) % 2)
    by_row = np.stack([row_cos, row_sin], 1) / math.sqrt(height)
    row_forward = np.einsum("qph,wv->qpwhv", by_row, np.eye(cell))
    row_forward = row_forward.reshape(2 * count * cell, height * cell)

    device = np.arange(count)
    start = (width // cols) * (device % cols) + cell * (device // cols)
    column = start[:, None] + np.arange(cell)[None, :]
    wave = np.arange(half + 1)
    angle = 2.0 * np.pi * ((wave[:, None, None] * column[None]) % width) / width
    cosine = np.cos(angle)
    sine = np.sin(angle)
    sine[0] = 0.0
    sine[half] = 0.0
    weight = np.where((wave == 0) | (wave == half), 1.0, 2.0)[:, None, None]
    factor = 1.0 / math.sqrt(width)
    forward = np.zeros((2, 2, 2, pad_k, count, 2, cell))
    inverse = np.zeros((2, count, 2, cell, 2, 2, pad_k))
    used = slice(0, half + 1)
    forward[0, 0, 0, used, :, 0] = cosine
    forward[0, 1, 0, used, :, 0] = -sine
    forward[0, 0, 1, used, :, 1] = cosine
    forward[0, 1, 1, used, :, 1] = -sine
    for chosen, sign in ((0, 1.0), (1, -1.0)):
        forward[1, 0, chosen, used, :, 0] = cosine
        forward[1, 0, chosen, used, :, 1] = sign * sine
        forward[1, 1, chosen, used, :, 0] = -sine
        forward[1, 1, chosen, used, :, 1] = sign * cosine
    back_cos = np.moveaxis(weight * cosine, 0, -1)
    back_sin = np.moveaxis(weight * sine, 0, -1)
    inverse[0, :, 0, :, 0, 0, used] = back_cos
    inverse[0, :, 0, :, 1, 0, used] = -back_sin
    inverse[0, :, 1, :, 0, 1, used] = back_cos
    inverse[0, :, 1, :, 1, 1, used] = -back_sin
    for chosen, sign in ((0, 1.0), (1, -1.0)):
        inverse[1, :, 0, :, 0, chosen, used] = back_cos
        inverse[1, :, 0, :, 1, chosen, used] = -back_sin
        inverse[1, :, 1, :, 0, chosen, used] = sign * back_sin
        inverse[1, :, 1, :, 1, chosen, used] = sign * back_cos
    forward = (forward * factor).reshape(2, 4 * pad_k, 2 * count * cell)
    inverse = (inverse * factor).reshape(2, 2 * count * cell, 4 * pad_k)
    narrow = ml_dtypes.bfloat16
    return (
        row_forward.astype(narrow),
        np.ascontiguousarray(row_forward.T).astype(narrow),
        forward.astype(narrow),
        inverse.astype(narrow),
    )


def mm(left, right):
    return jnp.dot(left, right, preferred_element_type=jnp.float32)


def kernel(
    rows, cols,
    feat_h, l2l_h, g2l_h, l2g_h, win_h, wfu_h, wout_h, rowf_h, rowi_h, colf_h, coli_h,
    in_scale, in_shift, fu_scale, fu_shift, loc_scale, loc_shift, glo_scale, glo_shift,
    outl_h, outg_h,
    pad, l2l, g2l, l2g, win, wfu, wout, rowf, rowi, colf, coli,
    mixers, norms, send_a, recv_a, send_b, recv_b, send_c, recv_c, send_d, recv_d,
    edge_out, edge_in, near, wide, acc_local, acc_cross, outl, outg,
    load_sem, sa, ra, sb, rb, sc, rc, sd, rd, sh, rh, store_sem,
):
    f32, b16 = jnp.float32, jnp.bfloat16
    count = rows * cols
    row = lax.axis_index("rows")
    col = lax.axis_index("cols")
    me = row * cols + col
    tall, across = pad.shape[0] - 2, pad.shape[1]
    local = l2l.shape[2]
    spec = win.shape[1]
    cell = across // rows
    channels = pad.shape[2]
    pixels = tall * across

    barrier = pltpu.get_barrier_semaphore()

    def greet(i, carry):
        j = lax.rem(me + i, count)
        pl.semaphore_signal(
            barrier, inc=1, device_id=(j // cols, lax.rem(j, cols)), device_id_type=MESH
        )
        return carry

    variant = jnp.where(me == 0, 0, 1)
    loads = [
        pltpu.make_async_copy(source, target, load_sem.at[i])
        for i, (source, target) in enumerate(
            [
                (feat_h, pad.at[pl.ds(1, tall)]),
                (win_h, win),
                (rowf_h, rowf),
                (wfu_h, wfu),
                (colf_h.at[variant], colf),
                (coli_h.at[variant], coli),
                (rowi_h, rowi),
                (l2l_h, l2l),
                (g2l_h, g2l),
                (l2g_h, l2g),
                (wout_h, wout),
            ]
        )
    ]
    for load in loads:
        load.start()
    lax.fori_loop(1, count, greet, 0)

    loads[0].wait()
    loads[1].wait()
    inner = pad[1 : tall + 1, :, local:].reshape(pixels, channels - local)
    reduced = jnp.maximum(mm(inner, win[...]) * in_scale[...] + in_shift[...], 0.0)
    reduced = reduced.reshape(tall, across, spec)
    for j in range(rows):
        block = reduced[:, j * cell : (j + 1) * cell, :].reshape(tall * cell, spec)
        send_a[j] = block.astype(b16)
    pl.semaphore_wait(barrier, count - 1)

    def in_column(source, target, sent, got):
        def begin(i, carry):
            j = lax.rem(row + i, rows)
            pltpu.make_async_remote_copy(
                src_ref=source.at[j], dst_ref=target.at[row], send_sem=sent.at[j],
                recv_sem=got.at[row], device_id=(j, col), device_id_type=MESH,
            ).start()
            return carry

        lax.fori_loop(1, rows, begin, 0)
        target[row] = source[row]

    def in_column_wait(source, target, sent, got):
        def end(i, carry):
            j = lax.rem(row + i, rows)
            pltpu.make_async_remote_copy(
                src_ref=source.at[j], dst_ref=target.at[j], send_sem=sent.at[j],
                recv_sem=got.at[j], device_id=(j, col), device_id_type=MESH,
            ).wait()
            return carry

        lax.fori_loop(1, rows, end, 0)

    def everywhere(source, target, sent, got):
        def begin(i, carry):
            j = lax.rem(me + i, count)
            pltpu.make_async_remote_copy(
                src_ref=source.at[j], dst_ref=target.at[me], send_sem=sent.at[j],
                recv_sem=got.at[me], device_id=(j // cols, lax.rem(j, cols)),
                device_id_type=MESH,
            ).start()
            return carry

        lax.fori_loop(1, count, begin, 0)
        target[me] = source[me]

    def everywhere_wait(source, target, sent, got):
        def end(i, carry):
            j = lax.rem(me + i, count)
            pltpu.make_async_remote_copy(
                src_ref=source.at[j], dst_ref=target.at[j], send_sem=sent.at[j],
                recv_sem=got.at[j], device_id=(j // cols, lax.rem(j, cols)),
                device_id_type=MESH,
            ).wait()
            return carry

        lax.fori_loop(1, count, end, 0)

    in_column(send_a, recv_a, sa, ra)

    up, down = lax.rem(row + rows - 1, rows), lax.rem(row + 1, rows)
    left, right = lax.rem(col + cols - 1, cols), lax.rem(col + 1, cols)
    halo = [
        pltpu.make_async_remote_copy(
            src_ref=source, dst_ref=target, send_sem=sh.at[i], recv_sem=rh.at[i],
            device_id=place, device_id_type=MESH,
        )
        for i, (source, target, place) in enumerate(
            [
                (pad.at[1], pad.at[tall + 1], (up, col)),
                (pad.at[tall], pad.at[0], (down, col)),
                (edge_out.at[0], edge_in.at[1], (row, left)),
                (edge_out.at[1], edge_in.at[0], (row, right)),
            ]
        )
    ]
    halo[0].start()
    halo[1].start()

    loads[3].wait()
    both = 2 * spec
    for part_in in range(2):
        pick_row = (
            lax.broadcasted_iota(jnp.int32, (spec, both), 1)
            == 2 * lax.broadcasted_iota(jnp.int32, (spec, both), 0) + part_in
        )
        picked = mm(pick_row.astype(f32).astype(b16), wfu[...]).astype(b16)
        for part_out in range(2):
            pick_col = (
                lax.broadcasted_iota(jnp.int32, (both, spec), 0)
                == 2 * lax.broadcasted_iota(jnp.int32, (both, spec), 1) + part_out
            ).astype(f32)
            mixers[part_in, part_out] = mm(picked, pick_col.astype(b16)).astype(b16)
            if part_in == 0:
                pair = jnp.concatenate(
                    [
                        jnp.broadcast_to(fu_scale[...], (8, both)),
                        jnp.broadcast_to(fu_shift[...], (8, both)),
                    ],
                    axis=0,
                )
                norms[part_out] = jnp.dot(
                    pair, pick_col, precision=lax.Precision.HIGHEST, preferred_element_type=f32
                )

    loads[2].wait()
    in_column_wait(send_a, recv_a, sa, ra)
    spread = mm(rowf[...], recv_a[...].reshape(pixels, spec))
    send_b[...] = spread.astype(b16).reshape(send_b.shape)
    everywhere(send_b, recv_b, sb, rb)

    halo[0].wait()
    halo[1].wait()

    @pl.when(row == 0)
    def _():
        pad[0] = pad[2]

    @pl.when(row == rows - 1)
    def _():
        pad[tall + 1] = pad[tall - 1]

    edge_rows = edge_out.shape[1]
    place = lax.broadcasted_iota(jnp.int32, (edge_rows, channels), 0)
    columns = [jnp.zeros((edge_rows, channels), f32) for _ in range(4)]
    for p in range(tall + 2):
        first = pad[p, :16, :].astype(f32)
        last = pad[p, across - 16 :, :].astype(f32)
        found = (first[0:1], last[15:16], first[1:2], last[14:15])
        columns = [jnp.where(place == p, f, c) for f, c in zip(found, columns)]
    edge_out[0] = columns[0].astype(b16)
    edge_out[1] = columns[1].astype(b16)
    halo[2].start()
    halo[3].start()
    halo[2].wait()
    halo[3].wait()
    before = jnp.where(col == 0, columns[2], edge_in[0].astype(f32))
    after = jnp.where(col == cols - 1, columns[3], edge_in[1].astype(f32))
    spot = lax.broadcasted_iota(jnp.int32, (across, channels), 0)
    wide_channels = channels - local
    for p in range(tall + 2):
        here = pad[p].astype(f32)
        shifted = (
            jnp.where(spot == 0, before[p : p + 1], pltpu.roll(here, 1, 0)).astype(b16),
            pad[p],
            jnp.where(spot == across - 1, after[p : p + 1], pltpu.roll(here, across - 1, 0)).astype(
                b16
            ),
        )
        span = slice(p * across, (p + 1) * across)
        for s, value in enumerate(shifted):
            near[span, s * local : (s + 1) * local] = value[:, :local]
            wide[span, s * wide_channels : (s + 1) * wide_channels] = value[:, local:]

    def convolve(dy):
        span = slice(dy * across, dy * across + pixels)
        close = near[span]
        local_part = mm(close, l2l[dy]) + mm(wide[span], g2l[dy])
        cross_part = mm(close, l2g[dy])
        if dy == 0:
            acc_local[...] = local_part
            acc_cross[...] = cross_part
        else:
            acc_local[...] += local_part
            acc_cross[...] += cross_part

    for i in (7, 8, 9):
        loads[i].wait()
    convolve(0)

    loads[4].wait()
    loads[5].wait()
    everywhere_wait(send_b, recv_b, sb, rb)
    cells = mm(colf[...], recv_b[...].reshape(pixels, spec)).astype(b16)
    middle = cells.shape[0] // 2
    cells_real, cells_imag = cells[:middle], cells[middle:]
    mixed = []
    for part in range(2):
        total = mm(cells_real, mixers[0, part]) + mm(cells_imag, mixers[1, part])
        mixed.append(
            jnp.maximum(total * norms[part, 0:1, :] + norms[part, 8:9, :], 0.0).astype(b16)
        )
    returned = mm(coli[...], jnp.concatenate(mixed, axis=0))
    send_c[...] = returned.astype(b16).reshape(send_c.shape)
    everywhere(send_c, recv_c, sc, rc)

    convolve(1)
    loads[6].wait()
    everywhere_wait(send_c, recv_c, sc, rc)
    image = mm(rowi[...], recv_c[...].reshape(pixels, spec))
    send_d[...] = image.astype(b16).reshape(send_d.shape)
    in_column(send_d, recv_d, sd, rd)

    convolve(2)
    local_out = jnp.maximum(acc_local[...] * loc_scale[...] + loc_shift[...], 0.0)
    outl[...] = local_out.astype(b16).reshape(outl.shape)
    store_local = pltpu.make_async_copy(outl, outl_h, store_sem.at[0])
    store_local.start()

    loads[10].wait()
    in_column_wait(send_d, recv_d, sd, rd)
    blocks = [send_a[j].astype(f32) + recv_d[j].astype(f32) for j in range(rows)]
    joined = jnp.concatenate(
        [blocks[j][h * cell : (h + 1) * cell] for h in range(tall) for j in range(rows)], axis=0
    ).astype(b16)
    total = acc_cross[...] + mm(joined, wout[...])
    global_out = jnp.maximum(total * glo_scale[...] + glo_shift[...], 0.0)
    outg[...] = global_out.astype(b16).reshape(outg.shape)
    store_global = pltpu.make_async_copy(outg, outg_h, store_sem.at[1])
    store_global.start()
    store_local.wait()
    store_global.wait()


def fused(rows, cols, features, *rest):
    (
        w_l2l, w_g2l, w_l2g, w_in, in_scale, in_shift, w_fu, fu_scale, fu_shift, w_out,
        local_scale, local_shift, global_scale, global_shift,
    ) = rest
    tall, across, channels = features.shape
    count = rows * cols
    height, width = tall * rows, across * cols
    if tall != 8 or height != 2 * count or width != 8 * count or across != 8 * rows:
        return shards(features, *rest)
    b16, f32 = jnp.bfloat16, jnp.float32
    local, glob, spec = w_l2l.shape[2], w_l2g.shape[3], w_in.shape[1]
    pixels = tall * across
    cell = across // rows
    pad_k = -(-(width // 2 + 1) // 16) * 16
    table = [jnp.asarray(t) for t in tables(rows, cols, height, width, pad_k)]
    weights = [
        w_l2l.reshape(3, 3 * w_l2l.shape[2], local),
        w_g2l.reshape(3, 3 * w_g2l.shape[2], local),
        w_l2g.reshape(3, 3 * w_l2g.shape[2], glob),
        w_in, w_fu, w_out,
    ]
    vectors = [
        v.reshape(1, -1)
        for v in (
            in_scale, in_shift, fu_scale, fu_shift, local_scale, local_shift, global_scale,
            global_shift,
        )
    ]
    anywhere = pl.BlockSpec(memory_space=pl.ANY)
    inside = pl.BlockSpec(memory_space=pltpu.VMEM)
    V = pltpu.VMEM
    many = pltpu.SemaphoreType.DMA
    by_row = V((rows, tall * cell, spec), b16)
    by_device = V((count, 2 * cell, spec), b16)
    return pl.pallas_call(
        functools.partial(kernel, rows, cols),
        out_shape=(
            jax.ShapeDtypeStruct((tall, across, local), b16),
            jax.ShapeDtypeStruct((tall, across, glob), b16),
        ),
        in_specs=[anywhere] * 11 + [inside] * 8,
        out_specs=(anywhere, anywhere),
        scratch_shapes=[
            V((tall + 2, across, channels), b16),
            *[V(w.shape, b16) for w in weights],
            V(table[0].shape, b16),
            V(table[1].shape, b16),
            V(table[2].shape[1:], b16),
            V(table[3].shape[1:], b16),
            V((2, 2, spec, spec), b16),
            V((2, 16, spec), f32),
            by_row, by_row, by_device, by_device, by_device, by_device, by_row, by_row,
            V((2, 16, channels), b16),
            V((2, 16, channels), b16),
            V(((tall + 2) * across, 3 * local), b16),
            V(((tall + 2) * across, 3 * (channels - local)), b16),
            V((pixels, local), f32),
            V((pixels, glob), f32),
            V((tall, across, local), b16),
            V((tall, across, glob), b16),
            many((11,)),
            many((rows,)), many((rows,)),
            many((count,)), many((count,)),
            many((count,)), many((count,)),
            many((rows,)), many((rows,)),
            many((4,)), many((4,)),
            many((2,)),
        ],
        compiler_params=pltpu.CompilerParams(
            collective_id=0, has_side_effects=True, vmem_limit_bytes=56 * 1024 * 1024
        ),
    )(features, *weights, *table, *vectors)


def solution(mesh):
    placed = (
        P("rows", "cols", None),
        P(),
        P(),
        P(),
        P(),
        P(),
        P(),
        P(),
        P(),
        P(),
        P(),
        P(),
        P(),
        P(),
        P(),
    )
    return jax.shard_map(
        functools.partial(fused, mesh.shape["rows"], mesh.shape["cols"]),
        mesh=mesh,
        in_specs=placed,
        out_specs=(P("rows", "cols", None), P("rows", "cols", None)),
        check_vma=False,
    )
```

```python
import functools
import math

import jax
import jax.numpy as jnp
import ml_dtypes
import numpy as np
from jax import lax
from jax.experimental import pallas as pl
from jax.experimental.pallas import tpu as pltpu
from jax.sharding import PartitionSpec as P

MESH = pl.DeviceIdType.MESH


def padded_2(x, sides, width):
    for axis, dim in sides:
        size, length = (lax.axis_size(axis), x.shape[dim])
        up = [(i, (i + 1) % size) for i in range(size - 1)]
        down = [(j, i) for i, j in up]
        last = lax.slice_in_dim(x, length - width, length, axis=dim)
        initial = lax.slice_in_dim(x, 0, width, axis=dim)
        before = lax.ppermute(last, axis, up)
        after = lax.ppermute(initial, axis, down)
        x = jnp.concatenate([before, x, after], axis=dim)
    return x


def rounded(value):
    return lax.optimization_barrier(value.astype(jnp.bfloat16))


def mirror_rows(value):
    return jnp.roll(jnp.flip(value, 0), 1, 0)


def angle_grid(count_a, count_b, modulus):
    left_index = lax.broadcasted_iota(jnp.int32, (count_a, count_b), 0)
    right_index = lax.broadcasted_iota(jnp.int32, (count_a, count_b), 1)
    return (left_index * right_index % modulus).astype(jnp.float32) * (2.0 * math.pi / modulus)


def along_rows(stacked, spectral, direction):
    highest = lax.Precision.HIGHEST
    length = stacked.shape[0]
    angles = angle_grid(length, length, length)
    factor = 1.0 / math.sqrt(length)
    cos_part = jnp.einsum("qh,hkc->qkc", jnp.cos(angles), stacked, precision=highest)
    sin_part = jnp.einsum("qh,hkc->qkc", jnp.sin(angles), stacked, precision=highest)
    if direction < 0:
        out_real = cos_part[..., :spectral] + sin_part[..., spectral:]
        out_imag = cos_part[..., spectral:] - sin_part[..., :spectral]
    else:
        out_real = cos_part[..., :spectral] - sin_part[..., spectral:]
        out_imag = cos_part[..., spectral:] + sin_part[..., :spectral]
    return (out_real * factor, out_imag * factor)


def shards(
    features,
    w_l2l,
    w_g2l,
    w_l2g,
    w_in,
    in_scale,
    in_shift,
    w_fu,
    fu_scale,
    fu_shift,
    w_out,
    local_scale,
    local_shift,
    global_scale,
    global_shift,
):
    floating = jnp.float32
    highest = lax.Precision.HIGHEST
    rows_here, cols_here, channels = features.shape
    local_width = w_l2l.shape[2]
    global_width = w_l2g.shape[3]
    spectral = w_in.shape[1]
    row_count = lax.axis_size("rows")
    col_count = lax.axis_size("cols")
    row_slab = rows_here // col_count
    column_total = cols_here * col_count
    half_width = column_total // 2
    row_total = rows_here * row_count
    per_device = half_width // (row_count * col_count)
    width_factor = 1.0 / math.sqrt(column_total)
    padded = padded_2(features, (("rows", 0), ("cols", 1)), 1)
    at_top = lax.axis_index("rows") == 0
    at_bottom = lax.axis_index("rows") == row_count - 1
    at_left = lax.axis_index("cols") == 0
    at_right = lax.axis_index("cols") == col_count - 1
    is_first = jnp.logical_and(at_top, at_left)
    padded = padded.at[0].set(jnp.where(at_top, padded[2], padded[0]))
    padded = padded.at[-1].set(jnp.where(at_bottom, padded[-3], padded[-1]))
    padded = padded.at[:, 0].set(jnp.where(at_left, padded[:, 2], padded[:, 0]))
    padded = padded.at[:, -1].set(jnp.where(at_right, padded[:, -3], padded[:, -1]))
    projected = jnp.einsum(
        "hwi,io->hwo", features[..., local_width:], w_in, preferred_element_type=floating
    )
    reduced = rounded(jnp.maximum(projected * in_scale + in_shift, 0.0))
    spread = lax.all_to_all(
        reduced.reshape(col_count, row_slab, cols_here, spectral),
        "cols",
        split_axis=0,
        concat_axis=2,
        tiled=True,
    )
    spread = spread.reshape(row_slab, column_total, spectral)
    pixel_index = lax.broadcasted_iota(jnp.int32, (column_total, half_width), 0)
    freq_index = lax.broadcasted_iota(jnp.int32, (column_total, half_width), 1)
    alternate = jnp.where(pixel_index % 2 == 0, 1.0, -1.0).astype(floating)
    forward_angles = angle_grid(column_total, half_width, column_total)
    forward_cos = jnp.cos(forward_angles)
    forward_sin = jnp.where(freq_index == 0, alternate, -jnp.sin(forward_angles))
    spread_float = spread.astype(floating)
    width_real = (
        jnp.einsum("hwc,wk->hkc", spread_float, forward_cos, precision=highest) * width_factor
    )
    width_imag = (
        jnp.einsum("hwc,wk->hkc", spread_float, forward_sin, precision=highest) * width_factor
    )
    width_spec = jnp.concatenate([width_real, width_imag], axis=-1).astype(jnp.bfloat16)
    width_spec = width_spec.reshape(1, row_slab, row_count, col_count, per_device, 2 * spectral)
    gathered = lax.all_to_all(
        lax.all_to_all(width_spec, "rows", split_axis=2, concat_axis=0, tiled=True),
        "cols",
        split_axis=3,
        concat_axis=1,
        tiled=True,
    )
    w_local = jnp.concatenate([w_l2l, w_g2l], axis=2)
    local_total = jnp.zeros((rows_here * cols_here, local_width), floating)
    cross_total = jnp.zeros((rows_here * cols_here, global_width), floating)
    for row_step in range(3):
        for col_step in range(3):
            window = padded[
                row_step : row_step + rows_here, col_step : col_step + cols_here
            ].reshape(-1, channels)
            local_total = local_total + jnp.dot(
                window, w_local[row_step, col_step], preferred_element_type=floating
            )
            cross_total = cross_total + jnp.dot(
                window[:, :local_width], w_l2g[row_step, col_step], preferred_element_type=floating
            )
    out_local = jnp.maximum(local_total * local_scale + local_shift, 0.0).astype(jnp.bfloat16)
    out_local = out_local.reshape(rows_here, cols_here, local_width)
    columns = gathered.reshape(row_total, per_device, 2 * spectral).astype(floating)
    spec_real, spec_imag = along_rows(columns, spectral, -1.0)
    spec_real = rounded(spec_real)
    spec_imag = rounded(spec_imag)
    first_real = spec_real[:, 0].astype(floating)
    first_imag = spec_imag[:, 0].astype(floating)
    mirror_real = mirror_rows(first_real)
    mirror_imag = mirror_rows(first_imag)
    zero_real = rounded((first_real + mirror_real) * 0.5)
    zero_imag = rounded((first_imag - mirror_imag) * 0.5)
    top_real = rounded((first_imag + mirror_imag) * 0.5)
    top_imag = rounded((mirror_real - first_real) * 0.5)
    lead_real = jnp.where(is_first, zero_real, spec_real[:, 0])
    lead_imag = jnp.where(is_first, zero_imag, spec_imag[:, 0])
    all_real = jnp.concatenate([lead_real[:, None], spec_real[:, 1:], top_real[:, None]], axis=1)
    all_imag = jnp.concatenate([lead_imag[:, None], spec_imag[:, 1:], top_imag[:, None]], axis=1)
    cells = jnp.concatenate([all_real, all_imag], axis=-1).reshape(
        row_total * (per_device + 1), 2 * spectral
    )
    reorder = jnp.concatenate([jnp.arange(spectral) * 2, jnp.arange(spectral) * 2 + 1])
    w_mix = w_fu[reorder][:, reorder]
    mixed_cells = rounded(
        jnp.maximum(
            jnp.dot(cells, w_mix, preferred_element_type=floating) * fu_scale[reorder]
            + fu_shift[reorder],
            0.0,
        )
    )
    mixed_grid = mixed_cells.reshape(row_total, per_device + 1, 2 * spectral).astype(floating)
    low_real = mixed_grid[:, 0, :spectral]
    low_imag = mixed_grid[:, 0, spectral:]
    high_real = mixed_grid[:, per_device, :spectral]
    high_imag = mixed_grid[:, per_device, spectral:]
    joint_real = (low_real + mirror_rows(low_real) - high_imag + mirror_rows(high_imag)) * 0.5
    joint_imag = (low_imag - mirror_rows(low_imag) + high_real + mirror_rows(high_real)) * 0.5
    joint = jnp.concatenate([joint_real, joint_imag], axis=-1)
    lead = jnp.where(is_first, joint, mixed_grid[:, 0])
    into = jnp.concatenate([lead[:, None], mixed_grid[:, 1:per_device]], axis=1)
    back_real, back_imag = along_rows(into, spectral, 1.0)
    back_rows = jnp.concatenate([back_real, back_imag], axis=-1).astype(jnp.bfloat16)
    back_rows = back_rows.reshape(row_total, 1, 1, per_device, 2 * spectral)
    returned = lax.all_to_all(
        lax.all_to_all(back_rows, "rows", split_axis=0, concat_axis=1, tiled=True),
        "cols",
        split_axis=0,
        concat_axis=2,
        tiled=True,
    )
    rows_grid = returned.reshape(row_slab, half_width, 2 * spectral).astype(floating)
    back_freq = lax.broadcasted_iota(jnp.int32, (half_width, column_total), 0)
    back_pixel = lax.broadcasted_iota(jnp.int32, (half_width, column_total), 1)
    back_alternate = jnp.where(back_pixel % 2 == 0, 1.0, -1.0).astype(floating)
    back_angles = angle_grid(half_width, column_total, column_total)
    back_cos = jnp.where(back_freq == 0, 1.0, 2.0 * jnp.cos(back_angles))
    back_sin = jnp.where(back_freq == 0, -back_alternate, 2.0 * jnp.sin(back_angles))
    fourier_real = jnp.einsum("hkc,kw->hwc", rows_grid[..., :spectral], back_cos, precision=highest)
    fourier_real = fourier_real - jnp.einsum(
        "hkc,kw->hwc", rows_grid[..., spectral:], back_sin, precision=highest
    )
    fourier = rounded(fourier_real * width_factor)
    joined = rounded(spread.astype(floating) + fourier.astype(floating))
    terms = jnp.einsum("hwc,co->hwo", joined, w_out, preferred_element_type=floating)
    terms = terms.reshape(row_slab, col_count, cols_here, global_width)
    projection = (
        lax.all_to_all(terms.astype(jnp.bfloat16), "cols", split_axis=1, concat_axis=0, tiled=True)
        .astype(terms.dtype)
        .reshape(rows_here, cols_here, global_width)
    )
    global_sum = cross_total.reshape(rows_here, cols_here, global_width) + projection
    out_global = jnp.maximum(global_sum * global_scale + global_shift, 0.0).astype(jnp.bfloat16)
    return (out_local, out_global)


def tables(rows, cols, height, width, pad_k):
    count = rows * cols
    cell = width // count
    half = width // 2
    freq = np.arange(count)[:, None]
    line = np.arange(height)[None, :]
    turn = 2.0 * np.pi * ((freq * line) % height) / height
    row_cos = np.cos(turn)
    row_sin = -np.sin(turn)
    row_sin[0] = 1.0 - 2.0 * (np.arange(height) % 2)
    by_row = np.stack([row_cos, row_sin], 1) / math.sqrt(height)
    row_forward = np.einsum("qph,wv->qpwhv", by_row, np.eye(cell))
    row_forward = row_forward.reshape(2 * count * cell, height * cell)

    device = np.arange(count)
    start = (width // cols) * (device % cols) + cell * (device // cols)
    column = start[:, None] + np.arange(cell)[None, :]
    wave = np.arange(half + 1)
    angle = 2.0 * np.pi * ((wave[:, None, None] * column[None]) % width) / width
    cosine = np.cos(angle)
    sine = np.sin(angle)
    sine[0] = 0.0
    sine[half] = 0.0
    weight = np.where((wave == 0) | (wave == half), 1.0, 2.0)[:, None, None]
    factor = 1.0 / math.sqrt(width)
    forward = np.zeros((2, 2, 2, pad_k, count, 2, cell))
    inverse = np.zeros((2, count, 2, cell, 2, 2, pad_k))
    used = slice(0, half + 1)
    forward[0, 0, 0, used, :, 0] = cosine
    forward[0, 1, 0, used, :, 0] = -sine
    forward[0, 0, 1, used, :, 1] = cosine
    forward[0, 1, 1, used, :, 1] = -sine
    for chosen, sign in ((0, 1.0), (1, -1.0)):
        forward[1, 0, chosen, used, :, 0] = cosine
        forward[1, 0, chosen, used, :, 1] = sign * sine
        forward[1, 1, chosen, used, :, 0] = -sine
        forward[1, 1, chosen, used, :, 1] = sign * cosine
    back_cos = np.moveaxis(weight * cosine, 0, -1)
    back_sin = np.moveaxis(weight * sine, 0, -1)
    inverse[0, :, 0, :, 0, 0, used] = back_cos
    inverse[0, :, 0, :, 1, 0, used] = -back_sin
    inverse[0, :, 1, :, 0, 1, used] = back_cos
    inverse[0, :, 1, :, 1, 1, used] = -back_sin
    for chosen, sign in ((0, 1.0), (1, -1.0)):
        inverse[1, :, 0, :, 0, chosen, used] = back_cos
        inverse[1, :, 0, :, 1, chosen, used] = -back_sin
        inverse[1, :, 1, :, 0, chosen, used] = sign * back_sin
        inverse[1, :, 1, :, 1, chosen, used] = sign * back_cos
    forward = (forward * factor).reshape(2, 4 * pad_k, 2 * count * cell)
    inverse = (inverse * factor).reshape(2, 2 * count * cell, 4 * pad_k)
    narrow = ml_dtypes.bfloat16
    return (
        row_forward.astype(narrow),
        np.ascontiguousarray(row_forward.T).astype(narrow),
        forward.astype(narrow),
        inverse.astype(narrow),
    )


def mm(left, right):
    return jnp.dot(left, right, preferred_element_type=jnp.float32)


def mm_nt(left, right):
    return lax.dot_general(
        left, right, (((1,), (1,)), ((), ())), preferred_element_type=jnp.float32
    )


def line(vector):
    return vector[...].reshape(1, vector.shape[0])


def hand_over(first, second, first_out, second_out, sems):
    copies = [
        pltpu.make_async_copy(first, first_out, sems.at[0]),
        pltpu.make_async_copy(second, second_out, sems.at[1]),
    ]
    for copy in copies:
        copy.start()
    for copy in copies:
        copy.wait()


def kernel(
    rows, cols,
    feat_h, l2l_h, g2l_h, l2g_h, win_h, wfu_h, wout_h, rowf_h, rowi_h, colf_h, coli_h,
    in_scale, in_shift, fu_scale, fu_shift, loc_scale, loc_shift, glo_scale, glo_shift,
    outl, outg,
    pad, l2l, g2l, l2g, win, wfu, wout, rowf, rowi, colf, coli,
    mixers, norms, send_a, recv_a, send_b, recv_b, send_c, recv_c, send_d, recv_d,
    edge_out, edge_in, near, wide, acc_local, acc_cross,
    load_sem, sa, ra, sb, rb, sc, rc, sd, rd, sh, rh,
):
    f32, b16 = jnp.float32, jnp.bfloat16
    count = rows * cols
    row = lax.axis_index("rows")
    col = lax.axis_index("cols")
    me = row * cols + col
    tall, across = pad.shape[0] - 2, pad.shape[1]
    local = l2l.shape[2]
    spec = win.shape[0]
    cell = across // rows
    channels = pad.shape[2]
    pixels = tall * across

    barrier = pltpu.get_barrier_semaphore()

    def greet(i, carry):
        j = lax.rem(me + i, count)
        pl.semaphore_signal(
            barrier, inc=1, device_id=(j // cols, lax.rem(j, cols)), device_id_type=MESH
        )
        return carry

    variant = jnp.where(me == 0, 0, 1)
    loads = [
        pltpu.make_async_copy(source, target, load_sem.at[i])
        for i, (source, target) in enumerate(
            [
                (feat_h, pad.at[pl.ds(1, tall)]),
                (win_h, win),
                (rowf_h, rowf),
                (wfu_h, wfu),
                (colf_h.at[variant], colf),
                (coli_h.at[variant], coli),
                (rowi_h, rowi),
                (l2l_h, l2l),
                (g2l_h, g2l),
                (l2g_h, l2g),
                (wout_h, wout),
            ]
        )
    ]
    for load in loads:
        load.start()
    lax.fori_loop(1, count, greet, 0)

    loads[0].wait()
    loads[1].wait()
    inner = pad[1 : tall + 1, :, local:].reshape(pixels, channels - local)
    reduced = jnp.maximum(mm_nt(inner, win[...]) * line(in_scale) + line(in_shift), 0.0)
    reduced = reduced.reshape(tall, across, spec)
    for j in range(rows):
        block = reduced[:, j * cell : (j + 1) * cell, :].reshape(tall * cell, spec)
        send_a[j] = block.astype(b16)
    pl.semaphore_wait(barrier, count - 1)

    def in_column(source, target, sent, got):
        def begin(i, carry):
            j = lax.rem(row + i, rows)
            pltpu.make_async_remote_copy(
                src_ref=source.at[j], dst_ref=target.at[row], send_sem=sent.at[j],
                recv_sem=got.at[row], device_id=(j, col), device_id_type=MESH,
            ).start()
            return carry

        lax.fori_loop(1, rows, begin, 0)
        target[row] = source[row]

    def in_column_wait(source, target, sent, got):
        def end(i, carry):
            j = lax.rem(row + i, rows)
            pltpu.make_async_remote_copy(
                src_ref=source.at[j], dst_ref=target.at[j], send_sem=sent.at[j],
                recv_sem=got.at[j], device_id=(j, col), device_id_type=MESH,
            ).wait()
            return carry

        lax.fori_loop(1, rows, end, 0)

    def everywhere(source, target, sent, got):
        def begin(i, carry):
            j = lax.rem(me + i, count)
            pltpu.make_async_remote_copy(
                src_ref=source.at[j], dst_ref=target.at[me], send_sem=sent.at[j],
                recv_sem=got.at[me], device_id=(j // cols, lax.rem(j, cols)),
                device_id_type=MESH,
            ).start()
            return carry

        lax.fori_loop(1, count, begin, 0)
        target[me] = source[me]

    def everywhere_wait(source, target, sent, got):
        def end(i, carry):
            j = lax.rem(me + i, count)
            pltpu.make_async_remote_copy(
                src_ref=source.at[j], dst_ref=target.at[j], send_sem=sent.at[j],
                recv_sem=got.at[j], device_id=(j // cols, lax.rem(j, cols)),
                device_id_type=MESH,
            ).wait()
            return carry

        lax.fori_loop(1, count, end, 0)

    in_column(send_a, recv_a, sa, ra)

    up, down = lax.rem(row + rows - 1, rows), lax.rem(row + 1, rows)
    left, right = lax.rem(col + cols - 1, cols), lax.rem(col + 1, cols)
    halo = [
        pltpu.make_async_remote_copy(
            src_ref=source, dst_ref=target, send_sem=sh.at[i], recv_sem=rh.at[i],
            device_id=place, device_id_type=MESH,
        )
        for i, (source, target, place) in enumerate(
            [
                (pad.at[1], pad.at[tall + 1], (up, col)),
                (pad.at[tall], pad.at[0], (down, col)),
                (edge_out.at[0], edge_in.at[1], (row, left)),
                (edge_out.at[1], edge_in.at[0], (row, right)),
            ]
        )
    ]
    halo[0].start()
    halo[1].start()

    loads[2].wait()
    in_column_wait(send_a, recv_a, sa, ra)
    spread = mm(rowf[...], recv_a[...].reshape(pixels, spec))
    send_b[...] = spread.astype(b16).reshape(send_b.shape)
    everywhere(send_b, recv_b, sb, rb)

    loads[3].wait()
    both = 2 * spec
    for part_in in range(2):
        pick_row = (
            lax.broadcasted_iota(jnp.int32, (spec, both), 1)
            == 2 * lax.broadcasted_iota(jnp.int32, (spec, both), 0) + part_in
        )
        picked = mm(pick_row.astype(f32).astype(b16), wfu[...]).astype(b16)
        for part_out in range(2):
            pick_col = (
                lax.broadcasted_iota(jnp.int32, (both, spec), 0)
                == 2 * lax.broadcasted_iota(jnp.int32, (both, spec), 1) + part_out
            ).astype(f32)
            mixers[part_in, part_out] = mm(picked, pick_col.astype(b16)).astype(b16)
            if part_in == 0:
                pair = jnp.concatenate(
                    [
                        jnp.broadcast_to(line(fu_scale), (8, both)),
                        jnp.broadcast_to(line(fu_shift), (8, both)),
                    ],
                    axis=0,
                )
                norms[part_out] = jnp.dot(
                    pair, pick_col, precision=lax.Precision.HIGHEST, preferred_element_type=f32
                )

    halo[0].wait()
    halo[1].wait()

    @pl.when(row == 0)
    def _():
        pad[0] = pad[2]

    @pl.when(row == rows - 1)
    def _():
        pad[tall + 1] = pad[tall - 1]

    edge_rows = edge_out.shape[1]
    place = lax.broadcasted_iota(jnp.int32, (edge_rows, channels), 0)
    columns = [jnp.zeros((edge_rows, channels), f32) for _ in range(4)]
    for p in range(tall + 2):
        first = pad[p, :16, :].astype(f32)
        last = pad[p, across - 16 :, :].astype(f32)
        found = (first[0:1], last[15:16], first[1:2], last[14:15])
        columns = [jnp.where(place == p, f, c) for f, c in zip(found, columns)]
    edge_out[0] = columns[0].astype(b16)
    edge_out[1] = columns[1].astype(b16)
    halo[2].start()
    halo[3].start()
    halo[2].wait()
    halo[3].wait()
    before = jnp.where(col == 0, columns[2], edge_in[0].astype(f32))
    after = jnp.where(col == cols - 1, columns[3], edge_in[1].astype(f32))
    spot = lax.broadcasted_iota(jnp.int32, (across, channels), 0)
    wide_channels = channels - local
    for p in range(tall + 2):
        here = pad[p].astype(f32)
        shifted = (
            jnp.where(spot == 0, before[p : p + 1], pltpu.roll(here, 1, 0)).astype(b16),
            pad[p],
            jnp.where(spot == across - 1, after[p : p + 1], pltpu.roll(here, across - 1, 0)).astype(
                b16
            ),
        )
        span = slice(p * across, (p + 1) * across)
        for s, value in enumerate(shifted):
            near[span, s * local : (s + 1) * local] = value[:, :local]
            wide[span, s * wide_channels : (s + 1) * wide_channels] = value[:, local:]

    def convolve(dy):
        span = slice(dy * across, dy * across + pixels)
        close = near[span]
        local_part = mm(close, l2l[dy]) + mm(wide[span], g2l[dy])
        cross_part = mm(close, l2g[dy])
        if dy == 0:
            acc_local[...] = local_part
            acc_cross[...] = cross_part
        else:
            acc_local[...] += local_part
            acc_cross[...] += cross_part

    for i in (7, 8, 9):
        loads[i].wait()
    convolve(0)

    loads[4].wait()
    loads[5].wait()
    everywhere_wait(send_b, recv_b, sb, rb)
    cells = mm(colf[...], recv_b[...].reshape(pixels, spec)).astype(b16)
    middle = cells.shape[0] // 2
    cells_real, cells_imag = cells[:middle], cells[middle:]
    mixed = []
    for part in range(2):
        total = mm(cells_real, mixers[0, part]) + mm(cells_imag, mixers[1, part])
        mixed.append(
            jnp.maximum(total * norms[part, 0:1, :] + norms[part, 8:9, :], 0.0).astype(b16)
        )
    returned = mm(coli[...], jnp.concatenate(mixed, axis=0))
    send_c[...] = returned.astype(b16).reshape(send_c.shape)
    everywhere(send_c, recv_c, sc, rc)

    convolve(1)
    loads[6].wait()
    everywhere_wait(send_c, recv_c, sc, rc)
    image = mm(rowi[...], recv_c[...].reshape(pixels, spec))
    send_d[...] = image.astype(b16).reshape(send_d.shape)
    in_column(send_d, recv_d, sd, rd)

    convolve(2)
    local_out = jnp.maximum(acc_local[...] * line(loc_scale) + line(loc_shift), 0.0)
    outl[...] = local_out.astype(b16).reshape(outl.shape)

    loads[10].wait()
    in_column_wait(send_d, recv_d, sd, rd)
    blocks = [send_a[j].astype(f32) + recv_d[j].astype(f32) for j in range(rows)]
    joined = jnp.concatenate(
        [blocks[j][h * cell : (h + 1) * cell] for h in range(tall) for j in range(rows)], axis=0
    ).astype(b16)
    total = acc_cross[...] + mm(joined, wout[...])
    global_out = jnp.maximum(total * line(glo_scale) + line(glo_shift), 0.0)
    outg[...] = global_out.astype(b16).reshape(outg.shape)


def fused(rows, cols, features, *rest):
    (
        w_l2l, w_g2l, w_l2g, w_in, in_scale, in_shift, w_fu, fu_scale, fu_shift, w_out,
        local_scale, local_shift, global_scale, global_shift,
    ) = rest
    tall, across, channels = features.shape
    count = rows * cols
    height, width = tall * rows, across * cols
    if tall != 8 or height != 2 * count or width != 8 * count or across != 8 * rows:
        return shards(features, *rest)
    b16, f32 = jnp.bfloat16, jnp.float32
    local, glob, spec = w_l2l.shape[2], w_l2g.shape[3], w_in.shape[1]
    pixels = tall * across
    cell = across // rows
    pad_k = -(-(width // 2 + 1) // 16) * 16
    table = [jnp.asarray(t) for t in tables(rows, cols, height, width, pad_k)]
    weights = [
        w_l2l.reshape(3, 3 * w_l2l.shape[2], local),
        w_g2l.reshape(3, 3 * w_g2l.shape[2], local),
        w_l2g.reshape(3, 3 * w_l2g.shape[2], glob),
        w_in.T, w_fu, w_out,
    ]
    vectors = [
        in_scale, in_shift, fu_scale, fu_shift, local_scale, local_shift, global_scale,
        global_shift,
    ]
    anywhere = pl.BlockSpec(memory_space=pl.ANY)
    inside = pl.BlockSpec(memory_space=pltpu.VMEM)
    V = pltpu.VMEM
    many = pltpu.SemaphoreType.DMA
    by_row = V((rows, tall * cell, spec), b16)
    by_device = V((count, 2 * cell, spec), b16)
    shapes = ((tall, across, local), (tall, across, glob))
    made = pl.pallas_call(
        functools.partial(kernel, rows, cols),
        out_shape=tuple(V(shape, b16) for shape in shapes),
        in_specs=[anywhere] * 11 + [inside] * 8,
        out_specs=(inside, inside),
        scratch_shapes=[
            V((tall + 2, across, channels), b16),
            *[V(w.shape, b16) for w in weights],
            V(table[0].shape, b16),
            V(table[1].shape, b16),
            V(table[2].shape[1:], b16),
            V(table[3].shape[1:], b16),
            V((2, 2, spec, spec), b16),
            V((2, 16, spec), f32),
            by_row, by_row, by_device, by_device, by_device, by_device, by_row, by_row,
            V((2, 16, channels), b16),
            V((2, 16, channels), b16),
            V(((tall + 2) * across, 3 * local), b16),
            V(((tall + 2) * across, 3 * (channels - local)), b16),
            V((pixels, local), f32),
            V((pixels, glob), f32),
            many((11,)),
            many((rows,)), many((rows,)),
            many((count,)), many((count,)),
            many((count,)), many((count,)),
            many((rows,)), many((rows,)),
            many((4,)), many((4,)),
        ],
        compiler_params=pltpu.CompilerParams(
            collective_id=0, has_side_effects=True, vmem_limit_bytes=56 * 1024 * 1024
        ),
    )(features, *weights, *table, *vectors)
    return pl.pallas_call(
        hand_over,
        out_shape=tuple(jax.ShapeDtypeStruct(shape, b16) for shape in shapes),
        in_specs=[inside, inside],
        out_specs=(anywhere, anywhere),
        scratch_shapes=[many((2,))],
    )(*made)


def solution(mesh):
    placed = (
        P("rows", "cols", None),
        P(),
        P(),
        P(),
        P(),
        P(),
        P(),
        P(),
        P(),
        P(),
        P(),
        P(),
        P(),
        P(),
        P(),
    )
    return jax.shard_map(
        functools.partial(fused, mesh.shape["rows"], mesh.shape["cols"]),
        mesh=mesh,
        in_specs=placed,
        out_specs=(P("rows", "cols", None), P("rows", "cols", None)),
        check_vma=False,
    )
```

```python
import functools
import math

import jax
import jax.numpy as jnp
import ml_dtypes
import numpy as np
from jax import lax
from jax.experimental import pallas as pl
from jax.experimental.pallas import tpu as pltpu
from jax.sharding import PartitionSpec as P

MESH = pl.DeviceIdType.MESH


def padded_2(x, sides, width):
    for axis, dim in sides:
        size, length = (lax.axis_size(axis), x.shape[dim])
        up = [(i, (i + 1) % size) for i in range(size - 1)]
        down = [(j, i) for i, j in up]
        last = lax.slice_in_dim(x, length - width, length, axis=dim)
        initial = lax.slice_in_dim(x, 0, width, axis=dim)
        before = lax.ppermute(last, axis, up)
        after = lax.ppermute(initial, axis, down)
        x = jnp.concatenate([before, x, after], axis=dim)
    return x


def rounded(value):
    return lax.optimization_barrier(value.astype(jnp.bfloat16))


def mirror_rows(value):
    return jnp.roll(jnp.flip(value, 0), 1, 0)


def angle_grid(count_a, count_b, modulus):
    left_index = lax.broadcasted_iota(jnp.int32, (count_a, count_b), 0)
    right_index = lax.broadcasted_iota(jnp.int32, (count_a, count_b), 1)
    return (left_index * right_index % modulus).astype(jnp.float32) * (2.0 * math.pi / modulus)


def along_rows(stacked, spectral, direction):
    highest = lax.Precision.HIGHEST
    length = stacked.shape[0]
    angles = angle_grid(length, length, length)
    factor = 1.0 / math.sqrt(length)
    cos_part = jnp.einsum("qh,hkc->qkc", jnp.cos(angles), stacked, precision=highest)
    sin_part = jnp.einsum("qh,hkc->qkc", jnp.sin(angles), stacked, precision=highest)
    if direction < 0:
        out_real = cos_part[..., :spectral] + sin_part[..., spectral:]
        out_imag = cos_part[..., spectral:] - sin_part[..., :spectral]
    else:
        out_real = cos_part[..., :spectral] - sin_part[..., spectral:]
        out_imag = cos_part[..., spectral:] + sin_part[..., :spectral]
    return (out_real * factor, out_imag * factor)


def shards(
    features,
    w_l2l,
    w_g2l,
    w_l2g,
    w_in,
    in_scale,
    in_shift,
    w_fu,
    fu_scale,
    fu_shift,
    w_out,
    local_scale,
    local_shift,
    global_scale,
    global_shift,
):
    floating = jnp.float32
    highest = lax.Precision.HIGHEST
    rows_here, cols_here, channels = features.shape
    local_width = w_l2l.shape[2]
    global_width = w_l2g.shape[3]
    spectral = w_in.shape[1]
    row_count = lax.axis_size("rows")
    col_count = lax.axis_size("cols")
    row_slab = rows_here // col_count
    column_total = cols_here * col_count
    half_width = column_total // 2
    row_total = rows_here * row_count
    per_device = half_width // (row_count * col_count)
    width_factor = 1.0 / math.sqrt(column_total)
    padded = padded_2(features, (("rows", 0), ("cols", 1)), 1)
    at_top = lax.axis_index("rows") == 0
    at_bottom = lax.axis_index("rows") == row_count - 1
    at_left = lax.axis_index("cols") == 0
    at_right = lax.axis_index("cols") == col_count - 1
    is_first = jnp.logical_and(at_top, at_left)
    padded = padded.at[0].set(jnp.where(at_top, padded[2], padded[0]))
    padded = padded.at[-1].set(jnp.where(at_bottom, padded[-3], padded[-1]))
    padded = padded.at[:, 0].set(jnp.where(at_left, padded[:, 2], padded[:, 0]))
    padded = padded.at[:, -1].set(jnp.where(at_right, padded[:, -3], padded[:, -1]))
    projected = jnp.einsum(
        "hwi,io->hwo", features[..., local_width:], w_in, preferred_element_type=floating
    )
    reduced = rounded(jnp.maximum(projected * in_scale + in_shift, 0.0))
    spread = lax.all_to_all(
        reduced.reshape(col_count, row_slab, cols_here, spectral),
        "cols",
        split_axis=0,
        concat_axis=2,
        tiled=True,
    )
    spread = spread.reshape(row_slab, column_total, spectral)
    pixel_index = lax.broadcasted_iota(jnp.int32, (column_total, half_width), 0)
    freq_index = lax.broadcasted_iota(jnp.int32, (column_total, half_width), 1)
    alternate = jnp.where(pixel_index % 2 == 0, 1.0, -1.0).astype(floating)
    forward_angles = angle_grid(column_total, half_width, column_total)
    forward_cos = jnp.cos(forward_angles)
    forward_sin = jnp.where(freq_index == 0, alternate, -jnp.sin(forward_angles))
    spread_float = spread.astype(floating)
    width_real = (
        jnp.einsum("hwc,wk->hkc", spread_float, forward_cos, precision=highest) * width_factor
    )
    width_imag = (
        jnp.einsum("hwc,wk->hkc", spread_float, forward_sin, precision=highest) * width_factor
    )
    width_spec = jnp.concatenate([width_real, width_imag], axis=-1).astype(jnp.bfloat16)
    width_spec = width_spec.reshape(1, row_slab, row_count, col_count, per_device, 2 * spectral)
    gathered = lax.all_to_all(
        lax.all_to_all(width_spec, "rows", split_axis=2, concat_axis=0, tiled=True),
        "cols",
        split_axis=3,
        concat_axis=1,
        tiled=True,
    )
    w_local = jnp.concatenate([w_l2l, w_g2l], axis=2)
    local_total = jnp.zeros((rows_here * cols_here, local_width), floating)
    cross_total = jnp.zeros((rows_here * cols_here, global_width), floating)
    for row_step in range(3):
        for col_step in range(3):
            window = padded[
                row_step : row_step + rows_here, col_step : col_step + cols_here
            ].reshape(-1, channels)
            local_total = local_total + jnp.dot(
                window, w_local[row_step, col_step], preferred_element_type=floating
            )
            cross_total = cross_total + jnp.dot(
                window[:, :local_width], w_l2g[row_step, col_step], preferred_element_type=floating
            )
    out_local = jnp.maximum(local_total * local_scale + local_shift, 0.0).astype(jnp.bfloat16)
    out_local = out_local.reshape(rows_here, cols_here, local_width)
    columns = gathered.reshape(row_total, per_device, 2 * spectral).astype(floating)
    spec_real, spec_imag = along_rows(columns, spectral, -1.0)
    spec_real = rounded(spec_real)
    spec_imag = rounded(spec_imag)
    first_real = spec_real[:, 0].astype(floating)
    first_imag = spec_imag[:, 0].astype(floating)
    mirror_real = mirror_rows(first_real)
    mirror_imag = mirror_rows(first_imag)
    zero_real = rounded((first_real + mirror_real) * 0.5)
    zero_imag = rounded((first_imag - mirror_imag) * 0.5)
    top_real = rounded((first_imag + mirror_imag) * 0.5)
    top_imag = rounded((mirror_real - first_real) * 0.5)
    lead_real = jnp.where(is_first, zero_real, spec_real[:, 0])
    lead_imag = jnp.where(is_first, zero_imag, spec_imag[:, 0])
    all_real = jnp.concatenate([lead_real[:, None], spec_real[:, 1:], top_real[:, None]], axis=1)
    all_imag = jnp.concatenate([lead_imag[:, None], spec_imag[:, 1:], top_imag[:, None]], axis=1)
    cells = jnp.concatenate([all_real, all_imag], axis=-1).reshape(
        row_total * (per_device + 1), 2 * spectral
    )
    reorder = jnp.concatenate([jnp.arange(spectral) * 2, jnp.arange(spectral) * 2 + 1])
    w_mix = w_fu[reorder][:, reorder]
    mixed_cells = rounded(
        jnp.maximum(
            jnp.dot(cells, w_mix, preferred_element_type=floating) * fu_scale[reorder]
            + fu_shift[reorder],
            0.0,
        )
    )
    mixed_grid = mixed_cells.reshape(row_total, per_device + 1, 2 * spectral).astype(floating)
    low_real = mixed_grid[:, 0, :spectral]
    low_imag = mixed_grid[:, 0, spectral:]
    high_real = mixed_grid[:, per_device, :spectral]
    high_imag = mixed_grid[:, per_device, spectral:]
    joint_real = (low_real + mirror_rows(low_real) - high_imag + mirror_rows(high_imag)) * 0.5
    joint_imag = (low_imag - mirror_rows(low_imag) + high_real + mirror_rows(high_real)) * 0.5
    joint = jnp.concatenate([joint_real, joint_imag], axis=-1)
    lead = jnp.where(is_first, joint, mixed_grid[:, 0])
    into = jnp.concatenate([lead[:, None], mixed_grid[:, 1:per_device]], axis=1)
    back_real, back_imag = along_rows(into, spectral, 1.0)
    back_rows = jnp.concatenate([back_real, back_imag], axis=-1).astype(jnp.bfloat16)
    back_rows = back_rows.reshape(row_total, 1, 1, per_device, 2 * spectral)
    returned = lax.all_to_all(
        lax.all_to_all(back_rows, "rows", split_axis=0, concat_axis=1, tiled=True),
        "cols",
        split_axis=0,
        concat_axis=2,
        tiled=True,
    )
    rows_grid = returned.reshape(row_slab, half_width, 2 * spectral).astype(floating)
    back_freq = lax.broadcasted_iota(jnp.int32, (half_width, column_total), 0)
    back_pixel = lax.broadcasted_iota(jnp.int32, (half_width, column_total), 1)
    back_alternate = jnp.where(back_pixel % 2 == 0, 1.0, -1.0).astype(floating)
    back_angles = angle_grid(half_width, column_total, column_total)
    back_cos = jnp.where(back_freq == 0, 1.0, 2.0 * jnp.cos(back_angles))
    back_sin = jnp.where(back_freq == 0, -back_alternate, 2.0 * jnp.sin(back_angles))
    fourier_real = jnp.einsum("hkc,kw->hwc", rows_grid[..., :spectral], back_cos, precision=highest)
    fourier_real = fourier_real - jnp.einsum(
        "hkc,kw->hwc", rows_grid[..., spectral:], back_sin, precision=highest
    )
    fourier = rounded(fourier_real * width_factor)
    joined = rounded(spread.astype(floating) + fourier.astype(floating))
    terms = jnp.einsum("hwc,co->hwo", joined, w_out, preferred_element_type=floating)
    terms = terms.reshape(row_slab, col_count, cols_here, global_width)
    projection = (
        lax.all_to_all(terms.astype(jnp.bfloat16), "cols", split_axis=1, concat_axis=0, tiled=True)
        .astype(terms.dtype)
        .reshape(rows_here, cols_here, global_width)
    )
    global_sum = cross_total.reshape(rows_here, cols_here, global_width) + projection
    out_global = jnp.maximum(global_sum * global_scale + global_shift, 0.0).astype(jnp.bfloat16)
    return (out_local, out_global)


def tables(rows, cols, height, width, pad_k):
    count = rows * cols
    cell = width // count
    half = width // 2
    freq = np.arange(count)[:, None]
    line = np.arange(height)[None, :]
    turn = 2.0 * np.pi * ((freq * line) % height) / height
    row_cos = np.cos(turn)
    row_sin = -np.sin(turn)
    row_sin[0] = 1.0 - 2.0 * (np.arange(height) % 2)
    by_row = np.stack([row_cos, row_sin], 1) / math.sqrt(height)
    row_forward = np.einsum("qph,wv->qpwhv", by_row, np.eye(cell))
    row_forward = row_forward.reshape(2 * count * cell, height * cell)

    device = np.arange(count)
    start = (width // cols) * (device % cols) + cell * (device // cols)
    column = start[:, None] + np.arange(cell)[None, :]
    wave = np.arange(half + 1)
    angle = 2.0 * np.pi * ((wave[:, None, None] * column[None]) % width) / width
    cosine = np.cos(angle)
    sine = np.sin(angle)
    sine[0] = 0.0
    sine[half] = 0.0
    weight = np.where((wave == 0) | (wave == half), 1.0, 2.0)[:, None, None]
    factor = 1.0 / math.sqrt(width)
    forward = np.zeros((2, 2, 2, pad_k, count, 2, cell))
    inverse = np.zeros((2, count, 2, cell, 2, 2, pad_k))
    used = slice(0, half + 1)
    forward[0, 0, 0, used, :, 0] = cosine
    forward[0, 1, 0, used, :, 0] = -sine
    forward[0, 0, 1, used, :, 1] = cosine
    forward[0, 1, 1, used, :, 1] = -sine
    for chosen, sign in ((0, 1.0), (1, -1.0)):
        forward[1, 0, chosen, used, :, 0] = cosine
        forward[1, 0, chosen, used, :, 1] = sign * sine
        forward[1, 1, chosen, used, :, 0] = -sine
        forward[1, 1, chosen, used, :, 1] = sign * cosine
    back_cos = np.moveaxis(weight * cosine, 0, -1)
    back_sin = np.moveaxis(weight * sine, 0, -1)
    inverse[0, :, 0, :, 0, 0, used] = back_cos
    inverse[0, :, 0, :, 1, 0, used] = -back_sin
    inverse[0, :, 1, :, 0, 1, used] = back_cos
    inverse[0, :, 1, :, 1, 1, used] = -back_sin
    for chosen, sign in ((0, 1.0), (1, -1.0)):
        inverse[1, :, 0, :, 0, chosen, used] = back_cos
        inverse[1, :, 0, :, 1, chosen, used] = -back_sin
        inverse[1, :, 1, :, 0, chosen, used] = sign * back_sin
        inverse[1, :, 1, :, 1, chosen, used] = sign * back_cos
    forward = (forward * factor).reshape(2, 4 * pad_k, 2 * count * cell)
    inverse = (inverse * factor).reshape(2, 2 * count * cell, 4 * pad_k)
    narrow = ml_dtypes.bfloat16
    return (
        row_forward.astype(narrow),
        np.ascontiguousarray(row_forward.T).astype(narrow),
        forward.astype(narrow),
        inverse.astype(narrow),
    )


def mm(left, right):
    return jnp.dot(left, right, preferred_element_type=jnp.float32)


def mm_nt(left, right):
    return lax.dot_general(
        left, right, (((1,), (1,)), ((), ())), preferred_element_type=jnp.float32
    )


def packed(value, groups):
    rows, wide = value.shape
    base = wide // 128 * 128
    half = rows // groups // 2
    low = value[:, :base].reshape(groups, 2 * half, base)
    high = value[:, base:].reshape(groups, 2, half, wide - base)
    high = jnp.concatenate([high[:, 0], high[:, 1]], axis=-1)
    return jnp.concatenate([low, high], axis=1).astype(jnp.bfloat16)


def unpacked(value):
    groups, rows, lanes = value.shape
    half = rows // 3
    low = value[:, : 2 * half].reshape(groups * 2 * half, lanes)
    high = value[:, 2 * half :].reshape(groups * half, lanes)
    turned = pltpu.roll(high, lanes // 2, 1)
    high = jnp.concatenate(
        [high.reshape(groups, 1, half, lanes), turned.reshape(groups, 1, half, lanes)], axis=1
    ).reshape(groups * 2 * half, lanes)
    return jnp.concatenate([low, high[:, : lanes // 2]], axis=1)


def line(vector):
    return vector[...].reshape(1, vector.shape[0])


def hand_over(first, second, first_out, second_out, sems):
    copies = [
        pltpu.make_async_copy(first, first_out, sems.at[0]),
        pltpu.make_async_copy(second, second_out, sems.at[1]),
    ]
    for copy in copies:
        copy.start()
    for copy in copies:
        copy.wait()


def kernel(
    rows, cols,
    feat_h, l2l_h, g2l_h, l2g_h, win_h, wfu_h, wout_h, rowf_h, rowi_h, colf_h, coli_h,
    in_scale, in_shift, fu_scale, fu_shift, loc_scale, loc_shift, glo_scale, glo_shift,
    outl, outg,
    pad, l2l, g2l, l2g, win, wfu, wout, rowf, rowi, colf, coli,
    mixers, norms, send_a, recv_a, send_b, recv_b, send_c, recv_c, send_d, recv_d,
    edge_out, edge_in, near, wide, acc_local, acc_cross,
    load_sem, sa, ra, sb, rb, sc, rc, sd, rd, sh, rh,
):
    f32, b16 = jnp.float32, jnp.bfloat16
    count = rows * cols
    row = lax.axis_index("rows")
    col = lax.axis_index("cols")
    me = row * cols + col
    tall, across = pad.shape[0] - 2, pad.shape[1]
    local = l2l.shape[2]
    spec = win.shape[0]
    cell = across // rows
    channels = pad.shape[2]
    pixels = tall * across

    barrier = pltpu.get_barrier_semaphore()

    def greet(i, carry):
        j = lax.rem(me + i, count)
        pl.semaphore_signal(
            barrier, inc=1, device_id=(j // cols, lax.rem(j, cols)), device_id_type=MESH
        )
        return carry

    variant = jnp.where(me == 0, 0, 1)
    loads = [
        pltpu.make_async_copy(source, target, load_sem.at[i])
        for i, (source, target) in enumerate(
            [
                (feat_h, pad.at[pl.ds(1, tall)]),
                (win_h, win),
                (rowf_h, rowf),
                (wfu_h, wfu),
                (colf_h.at[variant], colf),
                (coli_h.at[variant], coli),
                (rowi_h, rowi),
                (l2l_h, l2l),
                (g2l_h, g2l),
                (l2g_h, l2g),
                (wout_h, wout),
            ]
        )
    ]
    for load in loads[:3]:
        load.start()
    lax.fori_loop(1, count, greet, 0)

    loads[0].wait()
    loads[1].wait()
    inner = pad[1 : tall + 1, :, local:].reshape(pixels, channels - local)
    reduced = jnp.maximum(mm_nt(inner, win[...]) * line(in_scale) + line(in_shift), 0.0)
    reduced = reduced.reshape(tall, across, spec)
    by_block = [
        reduced[:, j * cell : (j + 1) * cell, :].reshape(tall * cell, spec) for j in range(rows)
    ]
    send_a[...] = packed(jnp.concatenate(by_block, axis=0), rows)
    for load in loads[3:]:
        load.start()
    pl.semaphore_wait(barrier, count - 1)

    def in_column(source, target, sent, got):
        def begin(i, carry):
            j = lax.rem(row + i, rows)
            pltpu.make_async_remote_copy(
                src_ref=source.at[j], dst_ref=target.at[row], send_sem=sent.at[j],
                recv_sem=got.at[row], device_id=(j, col), device_id_type=MESH,
            ).start()
            return carry

        lax.fori_loop(1, rows, begin, 0)
        target[row] = source[row]

    def in_column_wait(source, target, sent, got):
        def end(i, carry):
            j = lax.rem(row + i, rows)
            pltpu.make_async_remote_copy(
                src_ref=source.at[j], dst_ref=target.at[j], send_sem=sent.at[j],
                recv_sem=got.at[j], device_id=(j, col), device_id_type=MESH,
            ).wait()
            return carry

        lax.fori_loop(1, rows, end, 0)

    def everywhere(source, target, sent, got):
        def begin(i, carry):
            j = lax.rem(me + i, count)
            pltpu.make_async_remote_copy(
                src_ref=source.at[j], dst_ref=target.at[me], send_sem=sent.at[j],
                recv_sem=got.at[me], device_id=(j // cols, lax.rem(j, cols)),
                device_id_type=MESH,
            ).start()
            return carry

        lax.fori_loop(1, count, begin, 0)
        target[me] = source[me]

    def everywhere_wait(source, target, sent, got):
        def end(i, carry):
            j = lax.rem(me + i, count)
            pltpu.make_async_remote_copy(
                src_ref=source.at[j], dst_ref=target.at[j], send_sem=sent.at[j],
                recv_sem=got.at[j], device_id=(j // cols, lax.rem(j, cols)),
                device_id_type=MESH,
            ).wait()
            return carry

        lax.fori_loop(1, count, end, 0)

    in_column(send_a, recv_a, sa, ra)

    up, down = lax.rem(row + rows - 1, rows), lax.rem(row + 1, rows)
    left, right = lax.rem(col + cols - 1, cols), lax.rem(col + 1, cols)
    halo = [
        pltpu.make_async_remote_copy(
            src_ref=source, dst_ref=target, send_sem=sh.at[i], recv_sem=rh.at[i],
            device_id=place, device_id_type=MESH,
        )
        for i, (source, target, place) in enumerate(
            [
                (pad.at[1], pad.at[tall + 1], (up, col)),
                (pad.at[tall], pad.at[0], (down, col)),
                (edge_out.at[0], edge_in.at[1], (row, left)),
                (edge_out.at[1], edge_in.at[0], (row, right)),
            ]
        )
    ]
    halo[0].start()
    halo[1].start()

    loads[2].wait()
    in_column_wait(send_a, recv_a, sa, ra)
    spread = mm(rowf[...], unpacked(recv_a[...].astype(f32)).astype(b16))
    send_b[...] = packed(spread, count)
    everywhere(send_b, recv_b, sb, rb)

    loads[3].wait()
    both = 2 * spec
    for part_in in range(2):
        pick_row = (
            lax.broadcasted_iota(jnp.int32, (spec, both), 1)
            == 2 * lax.broadcasted_iota(jnp.int32, (spec, both), 0) + part_in
        )
        picked = mm(pick_row.astype(f32).astype(b16), wfu[...]).astype(b16)
        for part_out in range(2):
            pick_col = (
                lax.broadcasted_iota(jnp.int32, (both, spec), 0)
                == 2 * lax.broadcasted_iota(jnp.int32, (both, spec), 1) + part_out
            ).astype(f32)
            mixers[part_in, part_out] = mm(picked, pick_col.astype(b16)).astype(b16)
            if part_in == 0:
                pair = jnp.concatenate(
                    [
                        jnp.broadcast_to(line(fu_scale), (8, both)),
                        jnp.broadcast_to(line(fu_shift), (8, both)),
                    ],
                    axis=0,
                )
                norms[part_out] = jnp.dot(
                    pair, pick_col, precision=lax.Precision.HIGHEST, preferred_element_type=f32
                )

    halo[0].wait()
    halo[1].wait()

    @pl.when(row == 0)
    def _():
        pad[0] = pad[2]

    @pl.when(row == rows - 1)
    def _():
        pad[tall + 1] = pad[tall - 1]

    edge_rows = edge_out.shape[1]
    place = lax.broadcasted_iota(jnp.int32, (edge_rows, channels), 0)
    columns = [jnp.zeros((edge_rows, channels), f32) for _ in range(4)]
    for p in range(tall + 2):
        first = pad[p, :16, :].astype(f32)
        last = pad[p, across - 16 :, :].astype(f32)
        found = (first[0:1], last[15:16], first[1:2], last[14:15])
        columns = [jnp.where(place == p, f, c) for f, c in zip(found, columns)]
    edge_out[0] = columns[0].astype(b16)
    edge_out[1] = columns[1].astype(b16)
    halo[2].start()
    halo[3].start()
    halo[2].wait()
    halo[3].wait()
    before = jnp.where(col == 0, columns[2], edge_in[0].astype(f32))
    after = jnp.where(col == cols - 1, columns[3], edge_in[1].astype(f32))
    spot = lax.broadcasted_iota(jnp.int32, (across, channels), 0)
    wide_channels = channels - local
    for p in range(tall + 2):
        here = pad[p].astype(f32)
        shifted = (
            jnp.where(spot == 0, before[p : p + 1], pltpu.roll(here, 1, 0)).astype(b16),
            pad[p],
            jnp.where(spot == across - 1, after[p : p + 1], pltpu.roll(here, across - 1, 0)).astype(
                b16
            ),
        )
        span = slice(p * across, (p + 1) * across)
        for s, value in enumerate(shifted):
            near[span, s * local : (s + 1) * local] = value[:, :local]
            wide[span, s * wide_channels : (s + 1) * wide_channels] = value[:, local:]

    def convolve(dy):
        span = slice(dy * across, dy * across + pixels)
        close = near[span]
        local_part = mm(close, l2l[dy]) + mm(wide[span], g2l[dy])
        cross_part = mm(close, l2g[dy])
        if dy == 0:
            acc_local[...] = local_part
            acc_cross[...] = cross_part
        else:
            acc_local[...] += local_part
            acc_cross[...] += cross_part

    for i in (7, 8, 9):
        loads[i].wait()
    convolve(0)

    loads[4].wait()
    loads[5].wait()
    everywhere_wait(send_b, recv_b, sb, rb)
    cells = mm(colf[...], unpacked(recv_b[...].astype(f32)).astype(b16)).astype(b16)
    middle = cells.shape[0] // 2
    cells_real, cells_imag = cells[:middle], cells[middle:]
    mixed = []
    for part in range(2):
        total = mm(cells_real, mixers[0, part]) + mm(cells_imag, mixers[1, part])
        mixed.append(
            jnp.maximum(total * norms[part, 0:1, :] + norms[part, 8:9, :], 0.0).astype(b16)
        )
    returned = mm(coli[...], jnp.concatenate(mixed, axis=0))
    send_c[...] = packed(returned, count)
    everywhere(send_c, recv_c, sc, rc)

    convolve(1)
    loads[6].wait()
    everywhere_wait(send_c, recv_c, sc, rc)
    image = mm(rowi[...], unpacked(recv_c[...].astype(f32)).astype(b16))
    send_d[...] = packed(image, rows)
    in_column(send_d, recv_d, sd, rd)

    convolve(2)
    local_out = jnp.maximum(acc_local[...] * line(loc_scale) + line(loc_shift), 0.0)
    outl[...] = local_out.astype(b16).reshape(outl.shape)

    loads[10].wait()
    in_column_wait(send_d, recv_d, sd, rd)
    added = unpacked(send_a[...].astype(f32) + recv_d[...].astype(f32))
    blocks = [added[j * tall * cell : (j + 1) * tall * cell] for j in range(rows)]
    joined = jnp.concatenate(
        [blocks[j][h * cell : (h + 1) * cell] for h in range(tall) for j in range(rows)], axis=0
    ).astype(b16)
    total = acc_cross[...] + mm(joined, wout[...])
    global_out = jnp.maximum(total * line(glo_scale) + line(glo_shift), 0.0)
    outg[...] = global_out.astype(b16).reshape(outg.shape)


def fused(rows, cols, features, *rest):
    (
        w_l2l, w_g2l, w_l2g, w_in, in_scale, in_shift, w_fu, fu_scale, fu_shift, w_out,
        local_scale, local_shift, global_scale, global_shift,
    ) = rest
    tall, across, channels = features.shape
    count = rows * cols
    height, width = tall * rows, across * cols
    if tall != 8 or height != 2 * count or width != 8 * count or across != 8 * rows or w_in.shape[1] != 192:
        return shards(features, *rest)
    b16, f32 = jnp.bfloat16, jnp.float32
    local, glob, spec = w_l2l.shape[2], w_l2g.shape[3], w_in.shape[1]
    pixels = tall * across
    cell = across // rows
    pad_k = -(-(width // 2 + 1) // 16) * 16
    table = [jnp.asarray(t) for t in tables(rows, cols, height, width, pad_k)]
    weights = [
        w_l2l.reshape(3, 3 * w_l2l.shape[2], local),
        w_g2l.reshape(3, 3 * w_g2l.shape[2], local),
        w_l2g.reshape(3, 3 * w_l2g.shape[2], glob),
        w_in.T, w_fu, w_out,
    ]
    vectors = [
        in_scale, in_shift, fu_scale, fu_shift, local_scale, local_shift, global_scale,
        global_shift,
    ]
    anywhere = pl.BlockSpec(memory_space=pl.ANY)
    inside = pl.BlockSpec(memory_space=pltpu.VMEM)
    V = pltpu.VMEM
    many = pltpu.SemaphoreType.DMA
    by_row = V((rows, tall * cell * spec // 128, 128), b16)
    by_device = V((count, 2 * cell * spec // 128, 128), b16)
    shapes = ((tall, across, local), (tall, across, glob))
    made = pl.pallas_call(
        functools.partial(kernel, rows, cols),
        out_shape=tuple(V(shape, b16) for shape in shapes),
        in_specs=[anywhere] * 11 + [inside] * 8,
        out_specs=(inside, inside),
        scratch_shapes=[
            V((tall + 2, across, channels), b16),
            *[V(w.shape, b16) for w in weights],
            V(table[0].shape, b16),
            V(table[1].shape, b16),
            V(table[2].shape[1:], b16),
            V(table[3].shape[1:], b16),
            V((2, 2, spec, spec), b16),
            V((2, 16, spec), f32),
            by_row, by_row, by_device, by_device, by_device, by_device, by_row, by_row,
            V((2, 16, channels), b16),
            V((2, 16, channels), b16),
            V(((tall + 2) * across, 3 * local), b16),
            V(((tall + 2) * across, 3 * (channels - local)), b16),
            V((pixels, local), f32),
            V((pixels, glob), f32),
            many((11,)),
            many((rows,)), many((rows,)),
            many((count,)), many((count,)),
            many((count,)), many((count,)),
            many((rows,)), many((rows,)),
            many((4,)), many((4,)),
        ],
        compiler_params=pltpu.CompilerParams(
            collective_id=0, has_side_effects=True, vmem_limit_bytes=56 * 1024 * 1024
        ),
    )(features, *weights, *table, *vectors)
    return pl.pallas_call(
        hand_over,
        out_shape=tuple(jax.ShapeDtypeStruct(shape, b16) for shape in shapes),
        in_specs=[inside, inside],
        out_specs=(anywhere, anywhere),
        scratch_shapes=[many((2,))],
        compiler_params=pltpu.CompilerParams(vmem_limit_bytes=4 * 1024 * 1024),
    )(*made)


def solution(mesh):
    placed = (
        P("rows", "cols", None),
        P(),
        P(),
        P(),
        P(),
        P(),
        P(),
        P(),
        P(),
        P(),
        P(),
        P(),
        P(),
        P(),
        P(),
    )
    return jax.shard_map(
        functools.partial(fused, mesh.shape["rows"], mesh.shape["cols"]),
        mesh=mesh,
        in_specs=placed,
        out_specs=(P("rows", "cols", None), P("rows", "cols", None)),
        check_vma=False,
    )
```

```python
import functools
import math

import jax
import jax.numpy as jnp
import ml_dtypes
import numpy as np
from jax import lax
from jax.experimental import pallas as pl
from jax.experimental.pallas import tpu as pltpu
from jax.sharding import PartitionSpec as P

MESH = pl.DeviceIdType.MESH


def padded_2(x, sides, width):
    for axis, dim in sides:
        size, length = (lax.axis_size(axis), x.shape[dim])
        up = [(i, (i + 1) % size) for i in range(size - 1)]
        down = [(j, i) for i, j in up]
        last = lax.slice_in_dim(x, length - width, length, axis=dim)
        initial = lax.slice_in_dim(x, 0, width, axis=dim)
        before = lax.ppermute(last, axis, up)
        after = lax.ppermute(initial, axis, down)
        x = jnp.concatenate([before, x, after], axis=dim)
    return x


def rounded(value):
    return lax.optimization_barrier(value.astype(jnp.bfloat16))


def mirror_rows(value):
    return jnp.roll(jnp.flip(value, 0), 1, 0)


def angle_grid(count_a, count_b, modulus):
    left_index = lax.broadcasted_iota(jnp.int32, (count_a, count_b), 0)
    right_index = lax.broadcasted_iota(jnp.int32, (count_a, count_b), 1)
    return (left_index * right_index % modulus).astype(jnp.float32) * (2.0 * math.pi / modulus)


def along_rows(stacked, spectral, direction):
    highest = lax.Precision.HIGHEST
    length = stacked.shape[0]
    angles = angle_grid(length, length, length)
    factor = 1.0 / math.sqrt(length)
    cos_part = jnp.einsum("qh,hkc->qkc", jnp.cos(angles), stacked, precision=highest)
    sin_part = jnp.einsum("qh,hkc->qkc", jnp.sin(angles), stacked, precision=highest)
    if direction < 0:
        out_real = cos_part[..., :spectral] + sin_part[..., spectral:]
        out_imag = cos_part[..., spectral:] - sin_part[..., :spectral]
    else:
        out_real = cos_part[..., :spectral] - sin_part[..., spectral:]
        out_imag = cos_part[..., spectral:] + sin_part[..., :spectral]
    return (out_real * factor, out_imag * factor)


def shards(
    features,
    w_l2l,
    w_g2l,
    w_l2g,
    w_in,
    in_scale,
    in_shift,
    w_fu,
    fu_scale,
    fu_shift,
    w_out,
    local_scale,
    local_shift,
    global_scale,
    global_shift,
):
    floating = jnp.float32
    highest = lax.Precision.HIGHEST
    rows_here, cols_here, channels = features.shape
    local_width = w_l2l.shape[2]
    global_width = w_l2g.shape[3]
    spectral = w_in.shape[1]
    row_count = lax.axis_size("rows")
    col_count = lax.axis_size("cols")
    row_slab = rows_here // col_count
    column_total = cols_here * col_count
    half_width = column_total // 2
    row_total = rows_here * row_count
    per_device = half_width // (row_count * col_count)
    width_factor = 1.0 / math.sqrt(column_total)
    padded = padded_2(features, (("rows", 0), ("cols", 1)), 1)
    at_top = lax.axis_index("rows") == 0
    at_bottom = lax.axis_index("rows") == row_count - 1
    at_left = lax.axis_index("cols") == 0
    at_right = lax.axis_index("cols") == col_count - 1
    is_first = jnp.logical_and(at_top, at_left)
    padded = padded.at[0].set(jnp.where(at_top, padded[2], padded[0]))
    padded = padded.at[-1].set(jnp.where(at_bottom, padded[-3], padded[-1]))
    padded = padded.at[:, 0].set(jnp.where(at_left, padded[:, 2], padded[:, 0]))
    padded = padded.at[:, -1].set(jnp.where(at_right, padded[:, -3], padded[:, -1]))
    projected = jnp.einsum(
        "hwi,io->hwo", features[..., local_width:], w_in, preferred_element_type=floating
    )
    reduced = rounded(jnp.maximum(projected * in_scale + in_shift, 0.0))
    spread = lax.all_to_all(
        reduced.reshape(col_count, row_slab, cols_here, spectral),
        "cols",
        split_axis=0,
        concat_axis=2,
        tiled=True,
    )
    spread = spread.reshape(row_slab, column_total, spectral)
    pixel_index = lax.broadcasted_iota(jnp.int32, (column_total, half_width), 0)
    freq_index = lax.broadcasted_iota(jnp.int32, (column_total, half_width), 1)
    alternate = jnp.where(pixel_index % 2 == 0, 1.0, -1.0).astype(floating)
    forward_angles = angle_grid(column_total, half_width, column_total)
    forward_cos = jnp.cos(forward_angles)
    forward_sin = jnp.where(freq_index == 0, alternate, -jnp.sin(forward_angles))
    spread_float = spread.astype(floating)
    width_real = (
        jnp.einsum("hwc,wk->hkc", spread_float, forward_cos, precision=highest) * width_factor
    )
    width_imag = (
        jnp.einsum("hwc,wk->hkc", spread_float, forward_sin, precision=highest) * width_factor
    )
    width_spec = jnp.concatenate([width_real, width_imag], axis=-1).astype(jnp.bfloat16)
    width_spec = width_spec.reshape(1, row_slab, row_count, col_count, per_device, 2 * spectral)
    gathered = lax.all_to_all(
        lax.all_to_all(width_spec, "rows", split_axis=2, concat_axis=0, tiled=True),
        "cols",
        split_axis=3,
        concat_axis=1,
        tiled=True,
    )
    w_local = jnp.concatenate([w_l2l, w_g2l], axis=2)
    local_total = jnp.zeros((rows_here * cols_here, local_width), floating)
    cross_total = jnp.zeros((rows_here * cols_here, global_width), floating)
    for row_step in range(3):
        for col_step in range(3):
            window = padded[
                row_step : row_step + rows_here, col_step : col_step + cols_here
            ].reshape(-1, channels)
            local_total = local_total + jnp.dot(
                window, w_local[row_step, col_step], preferred_element_type=floating
            )
            cross_total = cross_total + jnp.dot(
                window[:, :local_width], w_l2g[row_step, col_step], preferred_element_type=floating
            )
    out_local = jnp.maximum(local_total * local_scale + local_shift, 0.0).astype(jnp.bfloat16)
    out_local = out_local.reshape(rows_here, cols_here, local_width)
    columns = gathered.reshape(row_total, per_device, 2 * spectral).astype(floating)
    spec_real, spec_imag = along_rows(columns, spectral, -1.0)
    spec_real = rounded(spec_real)
    spec_imag = rounded(spec_imag)
    first_real = spec_real[:, 0].astype(floating)
    first_imag = spec_imag[:, 0].astype(floating)
    mirror_real = mirror_rows(first_real)
    mirror_imag = mirror_rows(first_imag)
    zero_real = rounded((first_real + mirror_real) * 0.5)
    zero_imag = rounded((first_imag - mirror_imag) * 0.5)
    top_real = rounded((first_imag + mirror_imag) * 0.5)
    top_imag = rounded((mirror_real - first_real) * 0.5)
    lead_real = jnp.where(is_first, zero_real, spec_real[:, 0])
    lead_imag = jnp.where(is_first, zero_imag, spec_imag[:, 0])
    all_real = jnp.concatenate([lead_real[:, None], spec_real[:, 1:], top_real[:, None]], axis=1)
    all_imag = jnp.concatenate([lead_imag[:, None], spec_imag[:, 1:], top_imag[:, None]], axis=1)
    cells = jnp.concatenate([all_real, all_imag], axis=-1).reshape(
        row_total * (per_device + 1), 2 * spectral
    )
    reorder = jnp.concatenate([jnp.arange(spectral) * 2, jnp.arange(spectral) * 2 + 1])
    w_mix = w_fu[reorder][:, reorder]
    mixed_cells = rounded(
        jnp.maximum(
            jnp.dot(cells, w_mix, preferred_element_type=floating) * fu_scale[reorder]
            + fu_shift[reorder],
            0.0,
        )
    )
    mixed_grid = mixed_cells.reshape(row_total, per_device + 1, 2 * spectral).astype(floating)
    low_real = mixed_grid[:, 0, :spectral]
    low_imag = mixed_grid[:, 0, spectral:]
    high_real = mixed_grid[:, per_device, :spectral]
    high_imag = mixed_grid[:, per_device, spectral:]
    joint_real = (low_real + mirror_rows(low_real) - high_imag + mirror_rows(high_imag)) * 0.5
    joint_imag = (low_imag - mirror_rows(low_imag) + high_real + mirror_rows(high_real)) * 0.5
    joint = jnp.concatenate([joint_real, joint_imag], axis=-1)
    lead = jnp.where(is_first, joint, mixed_grid[:, 0])
    into = jnp.concatenate([lead[:, None], mixed_grid[:, 1:per_device]], axis=1)
    back_real, back_imag = along_rows(into, spectral, 1.0)
    back_rows = jnp.concatenate([back_real, back_imag], axis=-1).astype(jnp.bfloat16)
    back_rows = back_rows.reshape(row_total, 1, 1, per_device, 2 * spectral)
    returned = lax.all_to_all(
        lax.all_to_all(back_rows, "rows", split_axis=0, concat_axis=1, tiled=True),
        "cols",
        split_axis=0,
        concat_axis=2,
        tiled=True,
    )
    rows_grid = returned.reshape(row_slab, half_width, 2 * spectral).astype(floating)
    back_freq = lax.broadcasted_iota(jnp.int32, (half_width, column_total), 0)
    back_pixel = lax.broadcasted_iota(jnp.int32, (half_width, column_total), 1)
    back_alternate = jnp.where(back_pixel % 2 == 0, 1.0, -1.0).astype(floating)
    back_angles = angle_grid(half_width, column_total, column_total)
    back_cos = jnp.where(back_freq == 0, 1.0, 2.0 * jnp.cos(back_angles))
    back_sin = jnp.where(back_freq == 0, -back_alternate, 2.0 * jnp.sin(back_angles))
    fourier_real = jnp.einsum("hkc,kw->hwc", rows_grid[..., :spectral], back_cos, precision=highest)
    fourier_real = fourier_real - jnp.einsum(
        "hkc,kw->hwc", rows_grid[..., spectral:], back_sin, precision=highest
    )
    fourier = rounded(fourier_real * width_factor)
    joined = rounded(spread.astype(floating) + fourier.astype(floating))
    terms = jnp.einsum("hwc,co->hwo", joined, w_out, preferred_element_type=floating)
    terms = terms.reshape(row_slab, col_count, cols_here, global_width)
    projection = (
        lax.all_to_all(terms.astype(jnp.bfloat16), "cols", split_axis=1, concat_axis=0, tiled=True)
        .astype(terms.dtype)
        .reshape(rows_here, cols_here, global_width)
    )
    global_sum = cross_total.reshape(rows_here, cols_here, global_width) + projection
    out_global = jnp.maximum(global_sum * global_scale + global_shift, 0.0).astype(jnp.bfloat16)
    return (out_local, out_global)


def tables(rows, cols, height, width, pad_k):
    count = rows * cols
    cell = width // count
    half = width // 2
    freq = np.arange(count)[:, None]
    line = np.arange(height)[None, :]
    turn = 2.0 * np.pi * ((freq * line) % height) / height
    row_cos = np.cos(turn)
    row_sin = -np.sin(turn)
    row_sin[0] = 1.0 - 2.0 * (np.arange(height) % 2)
    by_row = np.stack([row_cos, row_sin], 1) / math.sqrt(height)
    row_forward = np.einsum("qph,wv->qpwhv", by_row, np.eye(cell))
    row_forward = row_forward.reshape(2 * count * cell, height * cell)

    device = np.arange(count)
    start = (width // cols) * (device % cols) + cell * (device // cols)
    column = start[:, None] + np.arange(cell)[None, :]
    wave = np.arange(half + 1)
    angle = 2.0 * np.pi * ((wave[:, None, None] * column[None]) % width) / width
    cosine = np.cos(angle)
    sine = np.sin(angle)
    sine[0] = 0.0
    sine[half] = 0.0
    weight = np.where((wave == 0) | (wave == half), 1.0, 2.0)[:, None, None]
    factor = 1.0 / math.sqrt(width)
    forward = np.zeros((2, 2, 2, pad_k, count, 2, cell))
    inverse = np.zeros((2, count, 2, cell, 2, 2, pad_k))
    used = slice(0, half + 1)
    forward[0, 0, 0, used, :, 0] = cosine
    forward[0, 1, 0, used, :, 0] = -sine
    forward[0, 0, 1, used, :, 1] = cosine
    forward[0, 1, 1, used, :, 1] = -sine
    for chosen, sign in ((0, 1.0), (1, -1.0)):
        forward[1, 0, chosen, used, :, 0] = cosine
        forward[1, 0, chosen, used, :, 1] = sign * sine
        forward[1, 1, chosen, used, :, 0] = -sine
        forward[1, 1, chosen, used, :, 1] = sign * cosine
    back_cos = np.moveaxis(weight * cosine, 0, -1)
    back_sin = np.moveaxis(weight * sine, 0, -1)
    inverse[0, :, 0, :, 0, 0, used] = back_cos
    inverse[0, :, 0, :, 1, 0, used] = -back_sin
    inverse[0, :, 1, :, 0, 1, used] = back_cos
    inverse[0, :, 1, :, 1, 1, used] = -back_sin
    for chosen, sign in ((0, 1.0), (1, -1.0)):
        inverse[1, :, 0, :, 0, chosen, used] = back_cos
        inverse[1, :, 0, :, 1, chosen, used] = -back_sin
        inverse[1, :, 1, :, 0, chosen, used] = sign * back_sin
        inverse[1, :, 1, :, 1, chosen, used] = sign * back_cos
    forward = (forward * factor).reshape(2, 4 * pad_k, 2 * count * cell)
    inverse = (inverse * factor).reshape(2, 2 * count * cell, 4 * pad_k)
    narrow = ml_dtypes.bfloat16
    return (
        row_forward.astype(narrow),
        np.ascontiguousarray(row_forward.T).astype(narrow),
        forward.astype(narrow),
        inverse.astype(narrow),
    )


def mm(left, right):
    return jnp.dot(left, right, preferred_element_type=jnp.float32)


def mm_nt(left, right):
    return lax.dot_general(
        left, right, (((1,), (1,)), ((), ())), preferred_element_type=jnp.float32
    )


def packed(value, groups):
    rows, wide = value.shape
    base = wide // 128 * 128
    half = rows // groups // 2
    low = value[:, :base].reshape(groups, 2 * half, base)
    high = value[:, base:].reshape(groups, 2, half, wide - base)
    high = jnp.concatenate([high[:, 0], high[:, 1]], axis=-1)
    return jnp.concatenate([low, high], axis=1).astype(jnp.bfloat16)


def unpacked(value):
    groups, rows, lanes = value.shape
    half = rows // 3
    low = value[:, : 2 * half].reshape(groups * 2 * half, lanes)
    high = value[:, 2 * half :].reshape(groups * half, lanes)
    turned = pltpu.roll(high, lanes // 2, 1)
    high = jnp.concatenate(
        [high.reshape(groups, 1, half, lanes), turned.reshape(groups, 1, half, lanes)], axis=1
    ).reshape(groups * 2 * half, lanes)
    return jnp.concatenate([low, high[:, : lanes // 2]], axis=1)


def line(vector):
    return vector[...].reshape(1, vector.shape[0])


def hand_over(first, second, first_out, second_out, sems):
    copies = [
        pltpu.make_async_copy(first, first_out, sems.at[0]),
        pltpu.make_async_copy(second, second_out, sems.at[1]),
    ]
    for copy in copies:
        copy.start()
    for copy in copies:
        copy.wait()


def kernel(
    rows, cols,
    feat_h, l2l_h, g2l_h, l2g_h, win_h, wfu_h, wout_h, rowf_h, rowi_h, colf_h, coli_h,
    in_scale, in_shift, fu_scale, fu_shift, loc_scale, loc_shift, glo_scale, glo_shift,
    outl, outg,
    pad, l2l, g2l, l2g, win, wfu, wout, rowf, rowi, colf, coli,
    mixers, norms, send_a, recv_a, send_b, recv_b, send_c, recv_c, send_d, recv_d,
    edge_out, edge_in, near, wide, acc_local, acc_cross,
    load_sem, sa, ra, sb, rb, sc, rc, sd, rd, sh, rh,
):
    f32, b16 = jnp.float32, jnp.bfloat16
    count = rows * cols
    row = lax.axis_index("rows")
    col = lax.axis_index("cols")
    me = row * cols + col
    tall, across = pad.shape[0] - 2, pad.shape[1]
    local = l2l.shape[2]
    spec = win.shape[0]
    cell = across // rows
    channels = pad.shape[2]
    pixels = tall * across

    barrier = pltpu.get_barrier_semaphore()

    def wrapped(index, size):
        return jnp.where(index >= size, index - size, index)

    ring = [wrapped(row + i, rows) for i in range(rows)]
    others = [
        (ring[a], wrapped(col + b, cols)) for a in range(rows) for b in range(cols) if a or b
    ]

    variant = jnp.where(me == 0, 0, 1)
    loads = [
        pltpu.make_async_copy(source, target, load_sem.at[i])
        for i, (source, target) in enumerate(
            [
                (feat_h, pad.at[pl.ds(1, tall)]),
                (win_h, win),
                (rowf_h, rowf),
                (wfu_h, wfu),
                (colf_h.at[variant], colf),
                (coli_h.at[variant], coli),
                (rowi_h, rowi),
                (l2l_h, l2l),
                (g2l_h, g2l),
                (l2g_h, l2g),
                (wout_h, wout),
            ]
        )
    ]
    for load in loads[:3]:
        load.start()
    for place in others:
        pl.semaphore_signal(barrier, inc=1, device_id=place, device_id_type=MESH)

    loads[0].wait()
    loads[1].wait()
    inner = pad[1 : tall + 1, :, local:].reshape(pixels, channels - local)
    reduced = jnp.maximum(mm_nt(inner, win[...]) * line(in_scale) + line(in_shift), 0.0)
    reduced = reduced.reshape(tall, across, spec)
    by_block = [
        reduced[:, j * cell : (j + 1) * cell, :].reshape(tall * cell, spec) for j in range(rows)
    ]
    send_a[...] = packed(jnp.concatenate(by_block, axis=0), rows)
    for load in loads[3:]:
        load.start()
    pl.semaphore_wait(barrier, count - 1)

    def push(source, target, sent, got, slot, place, mine):
        pltpu.make_async_remote_copy(
            src_ref=source.at[slot], dst_ref=target.at[mine], send_sem=sent.at[0],
            recv_sem=got.at[0], device_id=place, device_id_type=MESH,
        ).start()

    def in_column(source, target, sent, got):
        for j in ring[1:]:
            push(source, target, sent, got, j, (j, col), row)
        target[row] = source[row]

    def everywhere(source, target, sent, got):
        for there, beside in others:
            push(source, target, sent, got, there * cols + beside, (there, beside), me)
        target[me] = source[me]

    def all_of(buffer, sem):
        part = buffer.at[pl.ds(0, buffer.shape[0] - 1)]
        pltpu.make_async_copy(part, part, sem.at[0]).wait()

    in_column(send_a, recv_a, sa, ra)

    up, down = lax.rem(row + rows - 1, rows), lax.rem(row + 1, rows)
    left, right = lax.rem(col + cols - 1, cols), lax.rem(col + 1, cols)
    halo = [
        pltpu.make_async_remote_copy(
            src_ref=source, dst_ref=target, send_sem=sh.at[i], recv_sem=rh.at[i],
            device_id=place, device_id_type=MESH,
        )
        for i, (source, target, place) in enumerate(
            [
                (pad.at[1], pad.at[tall + 1], (up, col)),
                (pad.at[tall], pad.at[0], (down, col)),
                (edge_out.at[0], edge_in.at[1], (row, left)),
                (edge_out.at[1], edge_in.at[0], (row, right)),
            ]
        )
    ]
    halo[0].start()
    halo[1].start()

    loads[2].wait()
    all_of(recv_a, ra)
    spread = mm(rowf[...], unpacked(recv_a[...].astype(f32)).astype(b16))
    send_b[...] = packed(spread, count)
    everywhere(send_b, recv_b, sb, rb)

    loads[3].wait()
    both = 2 * spec
    for part_in in range(2):
        pick_row = (
            lax.broadcasted_iota(jnp.int32, (spec, both), 1)
            == 2 * lax.broadcasted_iota(jnp.int32, (spec, both), 0) + part_in
        )
        picked = mm(pick_row.astype(f32).astype(b16), wfu[...]).astype(b16)
        for part_out in range(2):
            pick_col = (
                lax.broadcasted_iota(jnp.int32, (both, spec), 0)
                == 2 * lax.broadcasted_iota(jnp.int32, (both, spec), 1) + part_out
            ).astype(f32)
            mixers[part_in, part_out] = mm(picked, pick_col.astype(b16)).astype(b16)
            if part_in == 0:
                pair = jnp.concatenate(
                    [
                        jnp.broadcast_to(line(fu_scale), (8, both)),
                        jnp.broadcast_to(line(fu_shift), (8, both)),
                    ],
                    axis=0,
                )
                norms[part_out] = jnp.dot(
                    pair, pick_col, precision=lax.Precision.HIGHEST, preferred_element_type=f32
                )

    halo[0].wait()
    halo[1].wait()

    @pl.when(row == 0)
    def _():
        pad[0] = pad[2]

    @pl.when(row == rows - 1)
    def _():
        pad[tall + 1] = pad[tall - 1]

    edge_rows = edge_out.shape[1]
    place = lax.broadcasted_iota(jnp.int32, (edge_rows, channels), 0)
    columns = [jnp.zeros((edge_rows, channels), f32) for _ in range(4)]
    for p in range(tall + 2):
        first = pad[p, :16, :].astype(f32)
        last = pad[p, across - 16 :, :].astype(f32)
        found = (first[0:1], last[15:16], first[1:2], last[14:15])
        columns = [jnp.where(place == p, f, c) for f, c in zip(found, columns)]
    edge_out[0] = columns[0].astype(b16)
    edge_out[1] = columns[1].astype(b16)
    halo[2].start()
    halo[3].start()
    halo[2].wait()
    halo[3].wait()
    before = jnp.where(col == 0, columns[2], edge_in[0].astype(f32))
    after = jnp.where(col == cols - 1, columns[3], edge_in[1].astype(f32))
    spot = lax.broadcasted_iota(jnp.int32, (across, channels), 0)
    wide_channels = channels - local
    for p in range(tall + 2):
        here = pad[p].astype(f32)
        shifted = (
            jnp.where(spot == 0, before[p : p + 1], pltpu.roll(here, 1, 0)).astype(b16),
            pad[p],
            jnp.where(spot == across - 1, after[p : p + 1], pltpu.roll(here, across - 1, 0)).astype(
                b16
            ),
        )
        span = slice(p * across, (p + 1) * across)
        for s, value in enumerate(shifted):
            near[span, s * local : (s + 1) * local] = value[:, :local]
            wide[span, s * wide_channels : (s + 1) * wide_channels] = value[:, local:]

    def convolve(dy):
        span = slice(dy * across, dy * across + pixels)
        close = near[span]
        local_part = mm(close, l2l[dy]) + mm(wide[span], g2l[dy])
        cross_part = mm(close, l2g[dy])
        if dy == 0:
            acc_local[...] = local_part
            acc_cross[...] = cross_part
        else:
            acc_local[...] += local_part
            acc_cross[...] += cross_part

    for i in (7, 8, 9):
        loads[i].wait()
    convolve(0)

    loads[4].wait()
    loads[5].wait()
    all_of(recv_b, rb)
    cells = mm(colf[...], unpacked(recv_b[...].astype(f32)).astype(b16)).astype(b16)
    middle = cells.shape[0] // 2
    cells_real, cells_imag = cells[:middle], cells[middle:]
    mixed = []
    for part in range(2):
        total = mm(cells_real, mixers[0, part]) + mm(cells_imag, mixers[1, part])
        mixed.append(
            jnp.maximum(total * norms[part, 0:1, :] + norms[part, 8:9, :], 0.0).astype(b16)
        )
    returned = mm(coli[...], jnp.concatenate(mixed, axis=0))
    send_c[...] = packed(returned, count)
    everywhere(send_c, recv_c, sc, rc)

    convolve(1)
    loads[6].wait()
    all_of(recv_c, rc)
    image = mm(rowi[...], unpacked(recv_c[...].astype(f32)).astype(b16))
    send_d[...] = packed(image, rows)
    in_column(send_d, recv_d, sd, rd)

    convolve(2)
    local_out = jnp.maximum(acc_local[...] * line(loc_scale) + line(loc_shift), 0.0)
    outl[...] = local_out.astype(b16).reshape(outl.shape)

    loads[10].wait()
    all_of(recv_d, rd)
    added = unpacked(send_a[...].astype(f32) + recv_d[...].astype(f32))
    blocks = [added[j * tall * cell : (j + 1) * tall * cell] for j in range(rows)]
    joined = jnp.concatenate(
        [blocks[j][h * cell : (h + 1) * cell] for h in range(tall) for j in range(rows)], axis=0
    ).astype(b16)
    total = acc_cross[...] + mm(joined, wout[...])
    global_out = jnp.maximum(total * line(glo_scale) + line(glo_shift), 0.0)
    outg[...] = global_out.astype(b16).reshape(outg.shape)
    for buffer, sem in ((send_a, sa), (send_b, sb), (send_c, sc), (send_d, sd)):
        all_of(buffer, sem)


def fused(rows, cols, features, *rest):
    (
        w_l2l, w_g2l, w_l2g, w_in, in_scale, in_shift, w_fu, fu_scale, fu_shift, w_out,
        local_scale, local_shift, global_scale, global_shift,
    ) = rest
    tall, across, channels = features.shape
    count = rows * cols
    height, width = tall * rows, across * cols
    if tall != 8 or height != 2 * count or width != 8 * count or across != 8 * rows or w_in.shape[1] != 192:
        return shards(features, *rest)
    b16, f32 = jnp.bfloat16, jnp.float32
    local, glob, spec = w_l2l.shape[2], w_l2g.shape[3], w_in.shape[1]
    pixels = tall * across
    cell = across // rows
    pad_k = -(-(width // 2 + 1) // 16) * 16
    table = [jnp.asarray(t) for t in tables(rows, cols, height, width, pad_k)]
    weights = [
        w_l2l.reshape(3, 3 * w_l2l.shape[2], local),
        w_g2l.reshape(3, 3 * w_g2l.shape[2], local),
        w_l2g.reshape(3, 3 * w_l2g.shape[2], glob),
        w_in.T, w_fu, w_out,
    ]
    vectors = [
        in_scale, in_shift, fu_scale, fu_shift, local_scale, local_shift, global_scale,
        global_shift,
    ]
    anywhere = pl.BlockSpec(memory_space=pl.ANY)
    inside = pl.BlockSpec(memory_space=pltpu.VMEM)
    V = pltpu.VMEM
    many = pltpu.SemaphoreType.DMA
    by_row = V((rows, tall * cell * spec // 128, 128), b16)
    by_device = V((count, 2 * cell * spec // 128, 128), b16)
    shapes = ((tall, across, local), (tall, across, glob))
    made = pl.pallas_call(
        functools.partial(kernel, rows, cols),
        out_shape=tuple(V(shape, b16) for shape in shapes),
        in_specs=[anywhere] * 11 + [inside] * 8,
        out_specs=(inside, inside),
        scratch_shapes=[
            V((tall + 2, across, channels), b16),
            *[V(w.shape, b16) for w in weights],
            V(table[0].shape, b16),
            V(table[1].shape, b16),
            V(table[2].shape[1:], b16),
            V(table[3].shape[1:], b16),
            V((2, 2, spec, spec), b16),
            V((2, 16, spec), f32),
            by_row, by_row, by_device, by_device, by_device, by_device, by_row, by_row,
            V((2, 16, channels), b16),
            V((2, 16, channels), b16),
            V(((tall + 2) * across, 3 * local), b16),
            V(((tall + 2) * across, 3 * (channels - local)), b16),
            V((pixels, local), f32),
            V((pixels, glob), f32),
            many((11,)),
            *[many((1,))] * 8,
            many((4,)), many((4,)),
        ],
        compiler_params=pltpu.CompilerParams(
            collective_id=0, has_side_effects=True, vmem_limit_bytes=56 * 1024 * 1024
        ),
    )(features, *weights, *table, *vectors)
    return pl.pallas_call(
        hand_over,
        out_shape=tuple(jax.ShapeDtypeStruct(shape, b16) for shape in shapes),
        in_specs=[inside, inside],
        out_specs=(anywhere, anywhere),
        scratch_shapes=[many((2,))],
        compiler_params=pltpu.CompilerParams(vmem_limit_bytes=4 * 1024 * 1024),
    )(*made)


def solution(mesh):
    placed = (
        P("rows", "cols", None),
        P(),
        P(),
        P(),
        P(),
        P(),
        P(),
        P(),
        P(),
        P(),
        P(),
        P(),
        P(),
        P(),
        P(),
    )
    return jax.shard_map(
        functools.partial(fused, mesh.shape["rows"], mesh.shape["cols"]),
        mesh=mesh,
        in_specs=placed,
        out_specs=(P("rows", "cols", None), P("rows", "cols", None)),
        check_vma=False,
    )
```

```python
import functools
import math

import jax
import jax.numpy as jnp
import ml_dtypes
import numpy as np
from jax import lax
from jax.experimental import pallas as pl
from jax.experimental.pallas import tpu as pltpu
from jax.sharding import PartitionSpec as P

MESH = pl.DeviceIdType.MESH


def padded_2(x, sides, width):
    for axis, dim in sides:
        size, length = (lax.axis_size(axis), x.shape[dim])
        up = [(i, (i + 1) % size) for i in range(size - 1)]
        down = [(j, i) for i, j in up]
        last = lax.slice_in_dim(x, length - width, length, axis=dim)
        initial = lax.slice_in_dim(x, 0, width, axis=dim)
        before = lax.ppermute(last, axis, up)
        after = lax.ppermute(initial, axis, down)
        x = jnp.concatenate([before, x, after], axis=dim)
    return x


def rounded(value):
    return lax.optimization_barrier(value.astype(jnp.bfloat16))


def mirror_rows(value):
    return jnp.roll(jnp.flip(value, 0), 1, 0)


def angle_grid(count_a, count_b, modulus):
    left_index = lax.broadcasted_iota(jnp.int32, (count_a, count_b), 0)
    right_index = lax.broadcasted_iota(jnp.int32, (count_a, count_b), 1)
    return (left_index * right_index % modulus).astype(jnp.float32) * (2.0 * math.pi / modulus)


def along_rows(stacked, spectral, direction):
    highest = lax.Precision.HIGHEST
    length = stacked.shape[0]
    angles = angle_grid(length, length, length)
    factor = 1.0 / math.sqrt(length)
    cos_part = jnp.einsum("qh,hkc->qkc", jnp.cos(angles), stacked, precision=highest)
    sin_part = jnp.einsum("qh,hkc->qkc", jnp.sin(angles), stacked, precision=highest)
    if direction < 0:
        out_real = cos_part[..., :spectral] + sin_part[..., spectral:]
        out_imag = cos_part[..., spectral:] - sin_part[..., :spectral]
    else:
        out_real = cos_part[..., :spectral] - sin_part[..., spectral:]
        out_imag = cos_part[..., spectral:] + sin_part[..., :spectral]
    return (out_real * factor, out_imag * factor)


def shards(
    features,
    w_l2l,
    w_g2l,
    w_l2g,
    w_in,
    in_scale,
    in_shift,
    w_fu,
    fu_scale,
    fu_shift,
    w_out,
    local_scale,
    local_shift,
    global_scale,
    global_shift,
):
    floating = jnp.float32
    highest = lax.Precision.HIGHEST
    rows_here, cols_here, channels = features.shape
    local_width = w_l2l.shape[2]
    global_width = w_l2g.shape[3]
    spectral = w_in.shape[1]
    row_count = lax.axis_size("rows")
    col_count = lax.axis_size("cols")
    row_slab = rows_here // col_count
    column_total = cols_here * col_count
    half_width = column_total // 2
    row_total = rows_here * row_count
    per_device = half_width // (row_count * col_count)
    width_factor = 1.0 / math.sqrt(column_total)
    padded = padded_2(features, (("rows", 0), ("cols", 1)), 1)
    at_top = lax.axis_index("rows") == 0
    at_bottom = lax.axis_index("rows") == row_count - 1
    at_left = lax.axis_index("cols") == 0
    at_right = lax.axis_index("cols") == col_count - 1
    is_first = jnp.logical_and(at_top, at_left)
    padded = padded.at[0].set(jnp.where(at_top, padded[2], padded[0]))
    padded = padded.at[-1].set(jnp.where(at_bottom, padded[-3], padded[-1]))
    padded = padded.at[:, 0].set(jnp.where(at_left, padded[:, 2], padded[:, 0]))
    padded = padded.at[:, -1].set(jnp.where(at_right, padded[:, -3], padded[:, -1]))
    projected = jnp.einsum(
        "hwi,io->hwo", features[..., local_width:], w_in, preferred_element_type=floating
    )
    reduced = rounded(jnp.maximum(projected * in_scale + in_shift, 0.0))
    spread = lax.all_to_all(
        reduced.reshape(col_count, row_slab, cols_here, spectral),
        "cols",
        split_axis=0,
        concat_axis=2,
        tiled=True,
    )
    spread = spread.reshape(row_slab, column_total, spectral)
    pixel_index = lax.broadcasted_iota(jnp.int32, (column_total, half_width), 0)
    freq_index = lax.broadcasted_iota(jnp.int32, (column_total, half_width), 1)
    alternate = jnp.where(pixel_index % 2 == 0, 1.0, -1.0).astype(floating)
    forward_angles = angle_grid(column_total, half_width, column_total)
    forward_cos = jnp.cos(forward_angles)
    forward_sin = jnp.where(freq_index == 0, alternate, -jnp.sin(forward_angles))
    spread_float = spread.astype(floating)
    width_real = (
        jnp.einsum("hwc,wk->hkc", spread_float, forward_cos, precision=highest) * width_factor
    )
    width_imag = (
        jnp.einsum("hwc,wk->hkc", spread_float, forward_sin, precision=highest) * width_factor
    )
    width_spec = jnp.concatenate([width_real, width_imag], axis=-1).astype(jnp.bfloat16)
    width_spec = width_spec.reshape(1, row_slab, row_count, col_count, per_device, 2 * spectral)
    gathered = lax.all_to_all(
        lax.all_to_all(width_spec, "rows", split_axis=2, concat_axis=0, tiled=True),
        "cols",
        split_axis=3,
        concat_axis=1,
        tiled=True,
    )
    w_local = jnp.concatenate([w_l2l, w_g2l], axis=2)
    local_total = jnp.zeros((rows_here * cols_here, local_width), floating)
    cross_total = jnp.zeros((rows_here * cols_here, global_width), floating)
    for row_step in range(3):
        for col_step in range(3):
            window = padded[
                row_step : row_step + rows_here, col_step : col_step + cols_here
            ].reshape(-1, channels)
            local_total = local_total + jnp.dot(
                window, w_local[row_step, col_step], preferred_element_type=floating
            )
            cross_total = cross_total + jnp.dot(
                window[:, :local_width], w_l2g[row_step, col_step], preferred_element_type=floating
            )
    out_local = jnp.maximum(local_total * local_scale + local_shift, 0.0).astype(jnp.bfloat16)
    out_local = out_local.reshape(rows_here, cols_here, local_width)
    columns = gathered.reshape(row_total, per_device, 2 * spectral).astype(floating)
    spec_real, spec_imag = along_rows(columns, spectral, -1.0)
    spec_real = rounded(spec_real)
    spec_imag = rounded(spec_imag)
    first_real = spec_real[:, 0].astype(floating)
    first_imag = spec_imag[:, 0].astype(floating)
    mirror_real = mirror_rows(first_real)
    mirror_imag = mirror_rows(first_imag)
    zero_real = rounded((first_real + mirror_real) * 0.5)
    zero_imag = rounded((first_imag - mirror_imag) * 0.5)
    top_real = rounded((first_imag + mirror_imag) * 0.5)
    top_imag = rounded((mirror_real - first_real) * 0.5)
    lead_real = jnp.where(is_first, zero_real, spec_real[:, 0])
    lead_imag = jnp.where(is_first, zero_imag, spec_imag[:, 0])
    all_real = jnp.concatenate([lead_real[:, None], spec_real[:, 1:], top_real[:, None]], axis=1)
    all_imag = jnp.concatenate([lead_imag[:, None], spec_imag[:, 1:], top_imag[:, None]], axis=1)
    cells = jnp.concatenate([all_real, all_imag], axis=-1).reshape(
        row_total * (per_device + 1), 2 * spectral
    )
    reorder = jnp.concatenate([jnp.arange(spectral) * 2, jnp.arange(spectral) * 2 + 1])
    w_mix = w_fu[reorder][:, reorder]
    mixed_cells = rounded(
        jnp.maximum(
            jnp.dot(cells, w_mix, preferred_element_type=floating) * fu_scale[reorder]
            + fu_shift[reorder],
            0.0,
        )
    )
    mixed_grid = mixed_cells.reshape(row_total, per_device + 1, 2 * spectral).astype(floating)
    low_real = mixed_grid[:, 0, :spectral]
    low_imag = mixed_grid[:, 0, spectral:]
    high_real = mixed_grid[:, per_device, :spectral]
    high_imag = mixed_grid[:, per_device, spectral:]
    joint_real = (low_real + mirror_rows(low_real) - high_imag + mirror_rows(high_imag)) * 0.5
    joint_imag = (low_imag - mirror_rows(low_imag) + high_real + mirror_rows(high_real)) * 0.5
    joint = jnp.concatenate([joint_real, joint_imag], axis=-1)
    lead = jnp.where(is_first, joint, mixed_grid[:, 0])
    into = jnp.concatenate([lead[:, None], mixed_grid[:, 1:per_device]], axis=1)
    back_real, back_imag = along_rows(into, spectral, 1.0)
    back_rows = jnp.concatenate([back_real, back_imag], axis=-1).astype(jnp.bfloat16)
    back_rows = back_rows.reshape(row_total, 1, 1, per_device, 2 * spectral)
    returned = lax.all_to_all(
        lax.all_to_all(back_rows, "rows", split_axis=0, concat_axis=1, tiled=True),
        "cols",
        split_axis=0,
        concat_axis=2,
        tiled=True,
    )
    rows_grid = returned.reshape(row_slab, half_width, 2 * spectral).astype(floating)
    back_freq = lax.broadcasted_iota(jnp.int32, (half_width, column_total), 0)
    back_pixel = lax.broadcasted_iota(jnp.int32, (half_width, column_total), 1)
    back_alternate = jnp.where(back_pixel % 2 == 0, 1.0, -1.0).astype(floating)
    back_angles = angle_grid(half_width, column_total, column_total)
    back_cos = jnp.where(back_freq == 0, 1.0, 2.0 * jnp.cos(back_angles))
    back_sin = jnp.where(back_freq == 0, -back_alternate, 2.0 * jnp.sin(back_angles))
    fourier_real = jnp.einsum("hkc,kw->hwc", rows_grid[..., :spectral], back_cos, precision=highest)
    fourier_real = fourier_real - jnp.einsum(
        "hkc,kw->hwc", rows_grid[..., spectral:], back_sin, precision=highest
    )
    fourier = rounded(fourier_real * width_factor)
    joined = rounded(spread.astype(floating) + fourier.astype(floating))
    terms = jnp.einsum("hwc,co->hwo", joined, w_out, preferred_element_type=floating)
    terms = terms.reshape(row_slab, col_count, cols_here, global_width)
    projection = (
        lax.all_to_all(terms.astype(jnp.bfloat16), "cols", split_axis=1, concat_axis=0, tiled=True)
        .astype(terms.dtype)
        .reshape(rows_here, cols_here, global_width)
    )
    global_sum = cross_total.reshape(rows_here, cols_here, global_width) + projection
    out_global = jnp.maximum(global_sum * global_scale + global_shift, 0.0).astype(jnp.bfloat16)
    return (out_local, out_global)


def tables(rows, cols, height, width, pad_k):
    count = rows * cols
    cell = width // count
    half = width // 2
    freq = np.arange(count)[:, None]
    line = np.arange(height)[None, :]
    turn = 2.0 * np.pi * ((freq * line) % height) / height
    row_cos = np.cos(turn)
    row_sin = -np.sin(turn)
    row_sin[0] = 1.0 - 2.0 * (np.arange(height) % 2)
    by_row = np.stack([row_cos, row_sin], 1) / math.sqrt(height)
    row_forward = np.einsum("qph,wv->qpwhv", by_row, np.eye(cell))
    row_forward = row_forward.reshape(2 * count * cell, height * cell)

    device = np.arange(count)
    start = (width // cols) * (device % cols) + cell * (device // cols)
    column = start[:, None] + np.arange(cell)[None, :]
    wave = np.arange(half + 1)
    angle = 2.0 * np.pi * ((wave[:, None, None] * column[None]) % width) / width
    cosine = np.cos(angle)
    sine = np.sin(angle)
    sine[0] = 0.0
    sine[half] = 0.0
    weight = np.where((wave == 0) | (wave == half), 1.0, 2.0)[:, None, None]
    factor = 1.0 / math.sqrt(width)
    forward = np.zeros((2, 2, 2, pad_k, count, 2, cell))
    inverse = np.zeros((2, count, 2, cell, 2, 2, pad_k))
    used = slice(0, half + 1)
    forward[0, 0, 0, used, :, 0] = cosine
    forward[0, 1, 0, used, :, 0] = -sine
    forward[0, 0, 1, used, :, 1] = cosine
    forward[0, 1, 1, used, :, 1] = -sine
    for chosen, sign in ((0, 1.0), (1, -1.0)):
        forward[1, 0, chosen, used, :, 0] = cosine
        forward[1, 0, chosen, used, :, 1] = sign * sine
        forward[1, 1, chosen, used, :, 0] = -sine
        forward[1, 1, chosen, used, :, 1] = sign * cosine
    back_cos = np.moveaxis(weight * cosine, 0, -1)
    back_sin = np.moveaxis(weight * sine, 0, -1)
    inverse[0, :, 0, :, 0, 0, used] = back_cos
    inverse[0, :, 0, :, 1, 0, used] = -back_sin
    inverse[0, :, 1, :, 0, 1, used] = back_cos
    inverse[0, :, 1, :, 1, 1, used] = -back_sin
    for chosen, sign in ((0, 1.0), (1, -1.0)):
        inverse[1, :, 0, :, 0, chosen, used] = back_cos
        inverse[1, :, 0, :, 1, chosen, used] = -back_sin
        inverse[1, :, 1, :, 0, chosen, used] = sign * back_sin
        inverse[1, :, 1, :, 1, chosen, used] = sign * back_cos
    forward = (forward * factor).reshape(2, 4 * pad_k, 2 * count * cell)
    inverse = (inverse * factor).reshape(2, 2 * count * cell, 4 * pad_k)
    narrow = ml_dtypes.bfloat16
    return (
        row_forward.astype(narrow),
        np.ascontiguousarray(row_forward.T).astype(narrow),
        forward.astype(narrow),
        inverse.astype(narrow),
    )


def mm(left, right):
    return jnp.dot(left, right, preferred_element_type=jnp.float32)


def mm_nt(left, right):
    return lax.dot_general(
        left, right, (((1,), (1,)), ((), ())), preferred_element_type=jnp.float32
    )


def packed(value, groups):
    rows, wide = value.shape
    base = wide // 128 * 128
    half = rows // groups // 2
    low = value[:, :base].reshape(groups, 2 * half, base)
    high = value[:, base:].reshape(groups, 2, half, wide - base)
    high = jnp.concatenate([high[:, 0], high[:, 1]], axis=-1)
    return jnp.concatenate([low, high], axis=1).astype(jnp.bfloat16)


def unpacked(value):
    groups, rows, lanes = value.shape
    half = rows // 3
    low = value[:, : 2 * half].reshape(groups * 2 * half, lanes)
    high = value[:, 2 * half :].reshape(groups * half, lanes)
    turned = pltpu.roll(high, lanes // 2, 1)
    high = jnp.concatenate(
        [high.reshape(groups, 1, half, lanes), turned.reshape(groups, 1, half, lanes)], axis=1
    ).reshape(groups * 2 * half, lanes)
    return jnp.concatenate([low, high[:, : lanes // 2]], axis=1)


def line(vector):
    return vector[...].reshape(1, vector.shape[0])


def hand_over(first, second, first_out, second_out, sems):
    copies = [
        pltpu.make_async_copy(first, first_out, sems.at[0]),
        pltpu.make_async_copy(second, second_out, sems.at[1]),
    ]
    for copy in copies:
        copy.start()
    for copy in copies:
        copy.wait()


def kernel(
    rows, cols,
    feat_h, l2l_h, g2l_h, l2g_h, win_h, wfu_h, wout_h, rowf_h, rowi_h, colf_h, coli_h,
    in_scale, in_shift, fu_scale, fu_shift, loc_scale, loc_shift, glo_scale, glo_shift,
    outl, outg,
    pad, l2l, g2l, l2g, win, wfu, wout, rowf, rowi, colf, coli,
    mixers, norms, send_a, recv_a, send_b, recv_b, send_c, recv_c, send_d, recv_d,
    edge_out, edge_in, near, wide, acc_local, acc_cross,
    load_sem, sa, ra, sb, rb, sc, rc, sd, rd, sh, rh,
):
    f32, b16 = jnp.float32, jnp.bfloat16
    count = rows * cols
    row = lax.axis_index("rows")
    col = lax.axis_index("cols")
    me = row * cols + col
    tall, across = pad.shape[0] - 2, pad.shape[1]
    local = l2l.shape[2]
    spec = win.shape[0]
    cell = across // rows
    channels = pad.shape[2]
    pixels = tall * across

    barrier = pltpu.get_barrier_semaphore()

    def wrapped(index, size):
        return jnp.where(index >= size, index - size, index)

    ring = [wrapped(row + i, rows) for i in range(rows)]
    others = [
        (ring[a], wrapped(col + b, cols)) for a in range(rows) for b in range(cols) if a or b
    ]

    variant = jnp.where(me == 0, 0, 1)
    loads = [
        pltpu.make_async_copy(source, target, load_sem.at[i])
        for i, (source, target) in enumerate(
            [
                (feat_h, pad.at[pl.ds(1, tall)]),
                (win_h, win),
                (rowf_h, rowf),
                (wfu_h, wfu),
                (colf_h.at[variant], colf),
                (coli_h.at[variant], coli),
                (rowi_h, rowi),
                (l2l_h, l2l),
                (g2l_h, g2l),
                (l2g_h, l2g),
                (wout_h, wout),
            ]
        )
    ]
    for load in loads[:3]:
        load.start()
    for place in others:
        pl.semaphore_signal(barrier, inc=1, device_id=place, device_id_type=MESH)

    loads[0].wait()
    loads[1].wait()
    inner = pad[1 : tall + 1, :, local:].reshape(pixels, channels - local)
    reduced = jnp.maximum(mm_nt(inner, win[...]) * line(in_scale) + line(in_shift), 0.0)
    reduced = reduced.reshape(tall, across, spec)
    by_block = [
        reduced[:, j * cell : (j + 1) * cell, :].reshape(tall * cell, spec) for j in range(rows)
    ]
    send_a[...] = packed(jnp.concatenate(by_block, axis=0), rows)
    for load in loads[3:]:
        load.start()
    pl.semaphore_wait(barrier, count - 1)

    def push(source, target, sent, got, slot, place, mine):
        pltpu.make_async_remote_copy(
            src_ref=source.at[slot], dst_ref=target.at[mine], send_sem=sent.at[0],
            recv_sem=got.at[0], device_id=place, device_id_type=MESH,
        ).start()

    def in_column(source, target, sent, got):
        for j in ring[1:]:
            push(source, target, sent, got, j, (j, col), row)
        target[row] = source[row]

    def everywhere(source, target, sent, got):
        for there, beside in others:
            push(source, target, sent, got, there * cols + beside, (there, beside), me)
        target[me] = source[me]

    def all_of(buffer, sem):
        part = buffer.at[pl.ds(0, buffer.shape[0] - 1)]
        pltpu.make_async_copy(part, part, sem.at[0]).wait()

    in_column(send_a, recv_a, sa, ra)

    up, down = lax.rem(row + rows - 1, rows), lax.rem(row + 1, rows)
    left, right = lax.rem(col + cols - 1, cols), lax.rem(col + 1, cols)
    halo = [
        pltpu.make_async_remote_copy(
            src_ref=source, dst_ref=target, send_sem=sh.at[i], recv_sem=rh.at[i],
            device_id=place, device_id_type=MESH,
        )
        for i, (source, target, place) in enumerate(
            [
                (pad.at[1], pad.at[tall + 1], (up, col)),
                (pad.at[tall], pad.at[0], (down, col)),
                (edge_out.at[0], edge_in.at[1], (row, left)),
                (edge_out.at[1], edge_in.at[0], (row, right)),
            ]
        )
    ]

    loads[2].wait()
    all_of(recv_a, ra)
    spread = mm(rowf[...], unpacked(recv_a[...].astype(f32)).astype(b16))
    send_b[...] = packed(spread, count)
    everywhere(send_b, recv_b, sb, rb)
    halo[0].start()
    halo[1].start()

    loads[3].wait()
    both = 2 * spec
    for part_in in range(2):
        pick_row = (
            lax.broadcasted_iota(jnp.int32, (spec, both), 1)
            == 2 * lax.broadcasted_iota(jnp.int32, (spec, both), 0) + part_in
        )
        picked = mm(pick_row.astype(f32).astype(b16), wfu[...]).astype(b16)
        for part_out in range(2):
            pick_col = (
                lax.broadcasted_iota(jnp.int32, (both, spec), 0)
                == 2 * lax.broadcasted_iota(jnp.int32, (both, spec), 1) + part_out
            ).astype(f32)
            mixers[part_in, part_out] = mm(picked, pick_col.astype(b16)).astype(b16)
            if part_in == 0:
                pair = jnp.concatenate(
                    [
                        jnp.broadcast_to(line(fu_scale), (8, both)),
                        jnp.broadcast_to(line(fu_shift), (8, both)),
                    ],
                    axis=0,
                )
                norms[part_out] = jnp.dot(
                    pair, pick_col, precision=lax.Precision.HIGHEST, preferred_element_type=f32
                )

    halo[0].wait()
    halo[1].wait()

    @pl.when(row == 0)
    def _():
        pad[0] = pad[2]

    @pl.when(row == rows - 1)
    def _():
        pad[tall + 1] = pad[tall - 1]

    edge_rows = edge_out.shape[1]
    place = lax.broadcasted_iota(jnp.int32, (edge_rows, channels), 0)
    columns = [jnp.zeros((edge_rows, channels), f32) for _ in range(4)]
    for p in range(tall + 2):
        first = pad[p, :16, :].astype(f32)
        last = pad[p, across - 16 :, :].astype(f32)
        found = (first[0:1], last[15:16], first[1:2], last[14:15])
        columns = [jnp.where(place == p, f, c) for f, c in zip(found, columns)]
    edge_out[0] = columns[0].astype(b16)
    edge_out[1] = columns[1].astype(b16)
    halo[2].start()
    halo[3].start()
    halo[2].wait()
    halo[3].wait()
    before = jnp.where(col == 0, columns[2], edge_in[0].astype(f32))
    after = jnp.where(col == cols - 1, columns[3], edge_in[1].astype(f32))
    spot = lax.broadcasted_iota(jnp.int32, (across, channels), 0)
    wide_channels = channels - local
    for p in range(tall + 2):
        here = pad[p].astype(f32)
        shifted = (
            jnp.where(spot == 0, before[p : p + 1], pltpu.roll(here, 1, 0)).astype(b16),
            pad[p],
            jnp.where(spot == across - 1, after[p : p + 1], pltpu.roll(here, across - 1, 0)).astype(
                b16
            ),
        )
        span = slice(p * across, (p + 1) * across)
        for s, value in enumerate(shifted):
            near[span, s * local : (s + 1) * local] = value[:, :local]
            wide[span, s * wide_channels : (s + 1) * wide_channels] = value[:, local:]

    def convolve(dy):
        span = slice(dy * across, dy * across + pixels)
        close = near[span]
        local_part = mm(close, l2l[dy]) + mm(wide[span], g2l[dy])
        cross_part = mm(close, l2g[dy])
        if dy == 0:
            acc_local[...] = local_part
            acc_cross[...] = cross_part
        else:
            acc_local[...] += local_part
            acc_cross[...] += cross_part

    for i in (7, 8, 9):
        loads[i].wait()
    convolve(0)

    loads[4].wait()
    loads[5].wait()
    all_of(recv_b, rb)
    cells = mm(colf[...], unpacked(recv_b[...].astype(f32)).astype(b16)).astype(b16)
    middle = cells.shape[0] // 2
    cells_real, cells_imag = cells[:middle], cells[middle:]
    mixed = []
    for part in range(2):
        total = mm(cells_real, mixers[0, part]) + mm(cells_imag, mixers[1, part])
        mixed.append(
            jnp.maximum(total * norms[part, 0:1, :] + norms[part, 8:9, :], 0.0).astype(b16)
        )
    returned = mm(coli[...], jnp.concatenate(mixed, axis=0))
    send_c[...] = packed(returned, count)
    everywhere(send_c, recv_c, sc, rc)

    convolve(1)
    loads[6].wait()
    all_of(recv_c, rc)
    image = mm(rowi[...], unpacked(recv_c[...].astype(f32)).astype(b16))
    send_d[...] = packed(image, rows)
    in_column(send_d, recv_d, sd, rd)

    convolve(2)
    local_out = jnp.maximum(acc_local[...] * line(loc_scale) + line(loc_shift), 0.0)
    outl[...] = local_out.astype(b16).reshape(outl.shape)

    loads[10].wait()
    all_of(recv_d, rd)
    added = unpacked(send_a[...].astype(f32) + recv_d[...].astype(f32))
    blocks = [added[j * tall * cell : (j + 1) * tall * cell] for j in range(rows)]
    joined = jnp.concatenate(
        [blocks[j][h * cell : (h + 1) * cell] for h in range(tall) for j in range(rows)], axis=0
    ).astype(b16)
    total = acc_cross[...] + mm(joined, wout[...])
    global_out = jnp.maximum(total * line(glo_scale) + line(glo_shift), 0.0)
    outg[...] = global_out.astype(b16).reshape(outg.shape)
    for buffer, sem in ((send_a, sa), (send_b, sb), (send_c, sc), (send_d, sd)):
        all_of(buffer, sem)


def fused(rows, cols, features, *rest):
    (
        w_l2l, w_g2l, w_l2g, w_in, in_scale, in_shift, w_fu, fu_scale, fu_shift, w_out,
        local_scale, local_shift, global_scale, global_shift,
    ) = rest
    tall, across, channels = features.shape
    count = rows * cols
    height, width = tall * rows, across * cols
    if tall != 8 or height != 2 * count or width != 8 * count or across != 8 * rows or w_in.shape[1] != 192:
        return shards(features, *rest)
    b16, f32 = jnp.bfloat16, jnp.float32
    local, glob, spec = w_l2l.shape[2], w_l2g.shape[3], w_in.shape[1]
    pixels = tall * across
    cell = across // rows
    pad_k = -(-(width // 2 + 1) // 16) * 16
    table = [jnp.asarray(t) for t in tables(rows, cols, height, width, pad_k)]
    weights = [
        w_l2l.reshape(3, 3 * w_l2l.shape[2], local),
        w_g2l.reshape(3, 3 * w_g2l.shape[2], local),
        w_l2g.reshape(3, 3 * w_l2g.shape[2], glob),
        w_in.T, w_fu, w_out,
    ]
    vectors = [
        in_scale, in_shift, fu_scale, fu_shift, local_scale, local_shift, global_scale,
        global_shift,
    ]
    anywhere = pl.BlockSpec(memory_space=pl.ANY)
    inside = pl.BlockSpec(memory_space=pltpu.VMEM)
    V = pltpu.VMEM
    many = pltpu.SemaphoreType.DMA
    by_row = V((rows, tall * cell * spec // 128, 128), b16)
    by_device = V((count, 2 * cell * spec // 128, 128), b16)
    shapes = ((tall, across, local), (tall, across, glob))
    made = pl.pallas_call(
        functools.partial(kernel, rows, cols),
        out_shape=tuple(V(shape, b16) for shape in shapes),
        in_specs=[anywhere] * 11 + [inside] * 8,
        out_specs=(inside, inside),
        scratch_shapes=[
            V((tall + 2, across, channels), b16),
            *[V(w.shape, b16) for w in weights],
            V(table[0].shape, b16),
            V(table[1].shape, b16),
            V(table[2].shape[1:], b16),
            V(table[3].shape[1:], b16),
            V((2, 2, spec, spec), b16),
            V((2, 16, spec), f32),
            by_row, by_row, by_device, by_device, by_device, by_device, by_row, by_row,
            V((2, 16, channels), b16),
            V((2, 16, channels), b16),
            V(((tall + 2) * across, 3 * local), b16),
            V(((tall + 2) * across, 3 * (channels - local)), b16),
            V((pixels, local), f32),
            V((pixels, glob), f32),
            many((11,)),
            *[many((1,))] * 8,
            many((4,)), many((4,)),
        ],
        compiler_params=pltpu.CompilerParams(
            collective_id=0, has_side_effects=True, vmem_limit_bytes=56 * 1024 * 1024
        ),
    )(features, *weights, *table, *vectors)
    return pl.pallas_call(
        hand_over,
        out_shape=tuple(jax.ShapeDtypeStruct(shape, b16) for shape in shapes),
        in_specs=[inside, inside],
        out_specs=(anywhere, anywhere),
        scratch_shapes=[many((2,))],
        compiler_params=pltpu.CompilerParams(vmem_limit_bytes=4 * 1024 * 1024),
    )(*made)


def solution(mesh):
    placed = (
        P("rows", "cols", None),
        P(),
        P(),
        P(),
        P(),
        P(),
        P(),
        P(),
        P(),
        P(),
        P(),
        P(),
        P(),
        P(),
        P(),
    )
    return jax.shard_map(
        functools.partial(fused, mesh.shape["rows"], mesh.shape["cols"]),
        mesh=mesh,
        in_specs=placed,
        out_specs=(P("rows", "cols", None), P("rows", "cols", None)),
        check_vma=False,
    )
```
